128 devices in a mesh: kvh: 8 (over z, x_hi), grp: 8 (over x_lo, y), blk: 2 (over core).
Axes of the slice: x: 4 (x_hi: 2, x_lo: 2; x = x_hi * 2 + x_lo), y: 4, z: 4, core: 2. Of those that a mesh axis runs over, the one named last changes fastest.
Arguments:
- queries: bfloat16 [32, 32, 16384], P(('grp', 'blk'), None, 'kvh'), may hold values from -30 to 30
- new_keys: bfloat16 [32, 32, 1024], P(('grp', 'blk'), None, 'kvh'), may hold values from -12 to 12
- new_values: bfloat16 [32, 32, 1024], P(('grp', 'blk'), None, 'kvh'), may hold values from -6 to 6
- prefix_keys: bfloat16 [16384, 1024], P(('grp', 'blk'), 'kvh'), may hold values from -8 to 8
- prefix_values: bfloat16 [16384, 1024], P(('grp', 'blk'), 'kvh'), may hold values from -6 to 6
- pool_keys: bfloat16 [512, 128, 1024], P(('grp', 'blk'), None, 'kvh'), may hold values from -7.1875 to 7.1875
- pool_values: bfloat16 [512, 128, 1024], P(('grp', 'blk'), None, 'kvh'), may hold values from -6 to 6
- hist_blocks: int32 [32, 16], replicated, may hold values from 0 to 511, as said below
- hist_len: int32 [32], replicated, may hold values from 1 to 2048
- out_weight: bfloat16 [16384, 16384], P('kvh', ('grp', 'blk')), may hold values from -0.046875 to 0.046875
Outputs:
- heads_out: bfloat16 [32, 32, 16384], P(('grp', 'blk'), None, 'kvh')
- projected: bfloat16 [32, 32, 16384], P('kvh', None, ('grp', 'blk'))
The draws below stay inside these ranges and needn't reach their ends.
Inputs may be any that keep to these rules, and one draw needn't show every extreme that they name: `hist_blocks`: block id b is row b mod 32 of the pool held by device b // 32 along grp+blk (grp slowest). Every pool block is named exactly once. The 2 requests placed on one device along grp+blk name exactly 2 blocks held by each device along grp+blk.
All inputs are finite; a program needn't handle non-finite values.
Results may differ from the reference program's by a relative error of at most 0.017.
Values may be sent and summed in bfloat16 or wider, within the bound.
A program may use at most 192 MiB of HBM per device.

```python
import jax
import jax.numpy as jnp
from jax import lax

HD = 128
GQ = 16
D = 16384
NEW = 32
BLK = 128
HIST = 2048
KVH = 8
NQH = 128
R = 32
PREFIX = 16384
NBLK = 16
POOL_DEV = 32
POOL = 512


def draw_queries(key, part):
    key = jax.random.fold_in(key, 21)
    first = jax.random.fold_in(key, 0)
    values = jnp.clip(5.0 * jax.random.normal(first, (R, NEW, NQH * HD), jnp.float32), -30.0, 30.0)
    return values.astype(jnp.bfloat16)


def draw_prefix_keys(key, part):
    key = jax.random.fold_in(key, 22)
    first = jax.random.fold_in(key, 0)
    values = jnp.clip(jax.random.normal(first, (PREFIX, KVH * HD), jnp.float32), -8.0, 8.0)
    return values.astype(jnp.bfloat16)


def permute_each(keys, length):
    return jax.vmap(lambda single: jax.random.permutation(single, length))(keys)


def draw_hist_blocks(key, part):
    key = jax.random.fold_in(key, 11)
    first, second = jax.random.split(key)
    holders = POOL // POOL_DEV
    per_holder = POOL_DEV // holders
    request_perm = permute_each(jax.random.split(first, holders), POOL_DEV)
    holder_of = request_perm % holders
    within = request_perm // holders
    holder_perm = permute_each(jax.random.split(second, holders), POOL_DEV)
    requester = jnp.arange(holders, dtype=jnp.int32)[:, None]
    local_ids = holder_perm[holder_of, requester * per_holder + within]
    block_ids = holder_of * POOL_DEV + local_ids
    return block_ids.reshape(R, NBLK).astype(jnp.int32)


def draw_hist_len(key, part):
    key = jax.random.fold_in(key, 12)
    first, second = jax.random.split(key)
    lengths = jax.random.randint(first, (R,), 1, HIST + 1, dtype=jnp.int32)
    chosen = jax.random.permutation(second, R)
    lengths = lengths.at[chosen[0]].set(HIST)
    lengths = lengths.at[chosen[1]].set(1)
    return lengths.astype(jnp.int32)


def shard_levels(own_key, extent, cuts, least, largest):
    gain, own = 1.0, jax.random.fold_in(own_key, 6)
    for axis_at, parts in cuts:
        heights = jnp.exp(jax.random.uniform(jax.random.fold_in(own, axis_at), (parts,), jnp.float32, least / len(cuts), largest / len(cuts)))
        gain = gain * jnp.repeat(heights, extent[axis_at] // parts).reshape([-1 if axis == axis_at else 1 for axis in range(len(extent))])
    return gain


def gaussian(stream_key, shape, width, bound, cuts=(), kind=jnp.bfloat16):
    array = jax.random.normal(stream_key, shape, jnp.float32) * width
    if len(cuts) > 0:
        array = shard_levels(stream_key, shape, cuts, -0.22, 0.18) * array
    return jnp.clip(array, min=-bound, max=bound).astype(kind)


def setup_inputs(seed: int = 0) -> dict:
    seeds = jax.random.split(jax.random.key(seed), 11)
    return {
        "queries": draw_queries(jax.random.fold_in(seeds[10], 71), 0),
        "new_keys": gaussian(seeds[1], (R, NEW, KVH * HD), 2.0, 12.0, ((0, 16), (2, 8))),
        "new_values": gaussian(seeds[2], (R, NEW, KVH * HD), 1.0, 6.0, ((0, 16), (2, 8))),
        "prefix_keys": draw_prefix_keys(jax.random.fold_in(seeds[10], 71), 0),
        "prefix_values": gaussian(seeds[4], (PREFIX, KVH * HD), 1.0, 6.0, ((0, 16), (1, 8))),
        "pool_keys": gaussian(seeds[5], (POOL, BLK, KVH * HD), 1.2, 7.1875, ((0, 16), (2, 8))),
        "pool_values": gaussian(seeds[6], (POOL, BLK, KVH * HD), 1.0, 6.0, ((0, 16), (2, 8))),
        "hist_blocks": draw_hist_blocks(jax.random.fold_in(seeds[10], 71), 0),
        "hist_len": draw_hist_len(jax.random.fold_in(seeds[10], 71), 0),
        "out_weight": gaussian(seeds[9], (NQH * HD, D), (NQH * HD) ** -0.5, 0.046875, ((0, 8), (1, 16))),
    }


def reference(queries, new_keys, new_values, prefix_keys, prefix_values, pool_keys, pool_values, hist_blocks, hist_len, out_weight):
    factor = HD ** -0.5
    zero_index = jnp.int32(0)

    def attend_pair(pair_index):
        head_group = pair_index // R
        request = pair_index % R
        query_rows = lax.dynamic_slice(queries, (request, zero_index, head_group * GQ * HD), (1, NEW, GQ * HD)).reshape(NEW * GQ, HD)
        pre_keys = lax.dynamic_slice_in_dim(prefix_keys, head_group * HD, HD, 1)
        pre_values = lax.dynamic_slice_in_dim(prefix_values, head_group * HD, HD, 1)
        block_ids = lax.dynamic_index_in_dim(hist_blocks, request, 0, keepdims=False)
        past_keys = lax.dynamic_slice_in_dim(jnp.take(pool_keys, block_ids, axis=0), head_group * HD, HD, 2).reshape(HIST, HD)
        past_values = lax.dynamic_slice_in_dim(jnp.take(pool_values, block_ids, axis=0), head_group * HD, HD, 2).reshape(HIST, HD)
        own_keys = lax.dynamic_slice(new_keys, (request, zero_index, head_group * HD), (1, NEW, HD))[0]
        own_values = lax.dynamic_slice(new_values, (request, zero_index, head_group * HD), (1, NEW, HD))[0]
        all_keys = jnp.concatenate([pre_keys, past_keys, own_keys], axis=0)
        all_values = jnp.concatenate([pre_values, past_values, own_values], axis=0)
        scores = jnp.dot(query_rows, all_keys.T, preferred_element_type=jnp.float32) * factor
        length = lax.dynamic_index_in_dim(hist_len, request, 0, keepdims=False)
        key_pos = jnp.arange(PREFIX + HIST + NEW, dtype=jnp.int32)
        query_tok = jnp.arange(NEW * GQ, dtype=jnp.int32) // GQ
        past_ok = (key_pos >= PREFIX) & (key_pos < PREFIX + HIST) & (key_pos - PREFIX < length)
        own_ok = (key_pos[None, :] >= PREFIX + HIST) & (key_pos[None, :] - PREFIX - HIST <= query_tok[:, None])
        visible = (key_pos[None, :] < PREFIX) | past_ok[None, :] | own_ok
        scores = jnp.where(visible, scores, jnp.float32(-1e30))
        top_score = jnp.max(scores, axis=1, keepdims=True)
        weights = jnp.where(visible, jnp.exp(scores - top_score), jnp.float32(0.0))
        total = jnp.sum(weights, axis=1, keepdims=True)
        summed = jnp.dot(weights.astype(jnp.bfloat16), all_values, preferred_element_type=jnp.float32)
        return (summed / total).astype(jnp.bfloat16).reshape(NEW, GQ * HD)

    results = lax.map(attend_pair, jnp.arange(KVH * R, dtype=jnp.int32))
    heads_out = results.reshape(KVH, R, NEW, GQ * HD).transpose(1, 2, 0, 3).reshape(R, NEW, NQH * HD)
    projected = jnp.dot(heads_out.reshape(R * NEW, NQH * HD), out_weight, preferred_element_type=jnp.float32)
    return heads_out, projected.astype(jnp.bfloat16).reshape(R, NEW, D)
```

```python
import functools
import math

import jax
import jax.numpy as jnp
from jax import lax
from jax.experimental import pallas as pl
from jax.experimental.pallas import tpu as pltpu
from jax.sharding import PartitionSpec as P

F32 = jnp.float32
BF16 = jnp.bfloat16
HEAD = 128
ROWS = 1024
TILE = 512
UNIT = 1024
ONES = 16
LOG2_SCALE = HEAD**-0.5 * math.log2(math.e)
HIDDEN = -1e30
NT = (((1,), (1,)), ((), ()))
VMEM_LIMIT = 60 * 2**20
VMEM = pl.BlockSpec(memory_space=pltpu.VMEM)
SMEM = pl.BlockSpec(memory_space=pltpu.SMEM)


def place():
    kvh, grp, core = lax.axis_index("kvh"), lax.axis_index("grp"), lax.axis_index("blk")
    return kvh, grp // 4, grp % 4, core


def peer(dx, dy, dc):
    kvh, x, y, core = place()
    px = 1 - x if dx else x
    pc = 1 - core if dc else core
    return (kvh, px * 4 + (y + dy) % 4, pc)


def remote(src, dst, send, recv, to):
    return pltpu.make_async_remote_copy(
        src_ref=src,
        dst_ref=dst,
        send_sem=send,
        recv_sem=recv,
        device_id=to,
        device_id_type=pl.DeviceIdType.MESH,
    )


def greet(peers):
    barrier = pltpu.get_barrier_semaphore()
    for to in peers:
        pl.semaphore_signal(barrier, inc=1, device_id=to, device_id_type=pl.DeviceIdType.MESH)
    pl.semaphore_wait(barrier, len(peers))


def turn(i):
    return jnp.where(i == 3, 0, 1 + (2 * i) % 3)


def attention_kernel(
    table,
    q_in,
    new_k,
    new_v,
    pre_k,
    pre_v,
    pool_k,
    pool_v,
    out,
    q_raw,
    q_two,
    kv,
    hist_out,
    hist,
    new_kv,
    top,
    accum,
    score_a,
    score_b,
    part_out,
    part_in,
    lse_out,
    lse_in,
    q_send,
    q_recv,
    kv_send,
    kv_recv,
    hist_send,
    hist_recv,
    part_send,
    part_recv,
    lse_send,
    lse_recv,
):
    kvh, x, y, core = place()
    partner = peer(0, 0, 1)
    scores = (score_a, score_b)

    def holder(t):
        dx, dc = t // 2, t % 2
        return ((1 - x if dx else x) * 4 + y) * 2 + (1 - core if dc else core)

    def entry(first_or_second, owner, request_pair):
        return table[first_or_second * 256 + owner * 16 + request_pair]

    def score(j, keys, tile, mask):
        count = keys.shape[0]
        value = lax.dot_general(
            jnp.concatenate([keys, keys], axis=1),
            q_two[j, tile * TILE : (tile + 1) * TILE, :],
            NT,
            preferred_element_type=F32,
        )
        if mask is None:
            scores[tile][:count] = value
        else:
            for b in range(count // 128):
                rows = slice(b * 128, (b + 1) * 128)
                scores[tile][rows] = jnp.where(mask(b, tile), value[rows], HIDDEN)

    def weigh(j, values, tile, count):
        cols = slice(tile * TILE, (tile + 1) * TILE)
        old = top[j, :, cols]
        newest = jnp.maximum(old, scores[tile][:count].max(axis=0, keepdims=True))
        shrink = jnp.exp2(old - newest)
        top[j, :, cols] = newest
        weights = jnp.exp2(scores[tile][:count] - newest).astype(BF16)
        values = jnp.concatenate([values, jnp.ones((ONES, count), BF16)], axis=0)
        accum[j, :, cols] = accum[j, :, cols] * shrink + jnp.dot(
            values, weights, preferred_element_type=F32
        )

    def absorb(j, parts):
        tasks = [(part, tile) for part in parts for tile in range(2)]
        score(j, tasks[0][0][0](), tasks[0][1], tasks[0][0][2])
        for at, ((keys, values, mask), tile) in enumerate(tasks):
            if at + 1 < len(tasks):
                (after_keys, _, after_mask), after_tile = tasks[at + 1]
                score(j, after_keys(), after_tile, after_mask)
            loaded = values()
            weigh(j, loaded, tile, loaded.shape[1])

    def prefix_part(slot):
        return (
            lambda: jnp.concatenate([kv[slot, 0, b] for b in range(8)], axis=0),
            lambda: jnp.concatenate([kv[slot, 1, b] for b in range(8)], axis=1),
            None,
        )

    def hist_part(j):
        request_pair = (x * 4 + (y + j) % 4) * 2 + core

        def mask(b, tile):
            code = entry(b % 2, holder(b // 2), request_pair)
            lane = lax.broadcasted_iota(jnp.int32, (1, TILE), 1)
            limit = jnp.where((lane // 32) % 2 == (code // 32) % 2, (code // 64) % 256, 0)
            return lax.broadcasted_iota(jnp.int32, (128, TILE), 0) < limit

        return (
            lambda: jnp.concatenate(
                [hist[t, j, 0, i] for t in range(4) for i in range(2)], axis=0
            ),
            lambda: jnp.concatenate(
                [hist[t, j, 1, i] for t in range(4) for i in range(2)], axis=1
            ),
            mask,
        )

    def new_part():
        def mask(b, tile):
            lane = lax.broadcasted_iota(jnp.int32, (128, TILE), 1) % 64
            key = lax.broadcasted_iota(jnp.int32, (128, TILE), 0)
            return (key <= lane) & (key >= (lane // 32) * 32)

        return (lambda: new_kv[0], lambda: new_kv[1], mask)

    def start_state(j):
        q = q_raw[j].astype(F32) * LOG2_SCALE
        high = q.astype(BF16)
        q_two[j, :, :HEAD] = high
        q_two[j, :, HEAD:] = (q - high.astype(F32)).astype(BF16)
        top[j] = jnp.full((1, ROWS), HIDDEN, F32)
        accum[j] = jnp.zeros((HEAD + ONES, ROWS), F32)

    for g in range(16):
        q_raw[0, g * 64 : (g + 1) * 64, :] = q_in[:, g * HEAD : (g + 1) * HEAD]
    for b in range(8):
        kv[0, 0, b] = pre_k[b * 128 : (b + 1) * 128, :]
        kv[0, 1, b] = pre_v[b * 128 : (b + 1) * 128, :].T

    greet([peer(0, 0, 1), peer(1, 0, 0), peer(1, 0, 1), peer(0, 1, 0), peer(0, 2, 0), peer(0, 3, 0)])

    def kv_copy(slot):
        src, to = ((0, partner), (0, peer(1, 0, 0)), (2, partner))[slot - 1]
        return remote(kv.at[src], kv.at[slot], kv_send.at[slot], kv_recv.at[slot], to)

    def q_copy(dy):
        to = peer(0, dy, 0)
        slot = (4 - dy) % 4
        return remote(q_raw.at[0], q_raw.at[slot], q_send.at[slot], q_recv.at[slot], to)

    def hist_copy(t, j):
        return remote(
            hist_out.at[t, j],
            hist.at[t, j],
            hist_send.at[t, j],
            hist_recv.at[t, j],
            peer(t // 2, 0, t % 2),
        )

    def part_copy(j):
        slot = (4 - j) % 4
        to = peer(0, j, 0)
        return (
            remote(part_out.at[j], part_in.at[slot], part_send.at[j], part_recv.at[slot], to),
            remote(lse_out.at[j], lse_in.at[slot], lse_send.at[j], lse_recv.at[slot], to),
        )

    kv_copy(2).start()
    kv_copy(1).start()
    for dy in (1, 3, 2):
        q_copy(dy).start()

    def fill(i, _):
        j = turn(i)
        for t in range(4):
            request_pair = (
                ((1 - x if t // 2 else x) * 4 + (y + j) % 4) * 2 + (1 - core if t % 2 else core)
            )
            own = (x * 4 + y) * 2 + core
            store = hist if t == 0 else hist_out
            for n in range(2):
                local = entry(n, own, request_pair) % 32
                store[t, j, 0, n] = pool_k[local]
                store[t, j, 1, n] = pool_v[local].T
            if t > 0:
                hist_copy(t, j).start()
        return 0

    lax.fori_loop(0, 4, fill, 0)

    start_state(0)
    new_kv[...] = jnp.zeros((2, 128, 128), BF16)
    new_kv[0, :64, :] = new_k[...]
    new_kv[1, :, :] = jnp.concatenate([new_v[...], jnp.zeros((64, HEAD), BF16)], axis=0).T
    absorb(0, [prefix_part(0), new_part()])
    kv_copy(1).wait_recv()
    absorb(0, [prefix_part(1)])

    def near(i, _):
        @pl.when(i == 2)
        def _():
            kv_copy(2).wait_recv()
            kv_copy(3).start()

        j = turn(i)
        remote(q_raw.at[0], q_raw.at[j], q_send.at[j], q_recv.at[j], partner).wait_recv()
        start_state(j)
        absorb(j, [prefix_part(0), prefix_part(1)])
        return 0

    lax.fori_loop(0, 3, near, 0)
    kv_copy(3).wait_recv()

    def far(i, _):
        j = turn(i)
        absorb(j, [prefix_part(2), prefix_part(3)])
        for t in range(1, 4):
            hist_copy(t, j).wait_recv()
        absorb(j, [hist_part(j)])

        @pl.when(i < 3)
        def _():
            total = accum[j, HEAD : HEAD + 1, :]
            part_out[j] = (accum[j, :HEAD, :] / total).astype(BF16)
            lse_out[j] = top[j] + jnp.log2(total)
            for copy in part_copy(j):
                copy.start()

        return 0

    lax.fori_loop(0, 4, far, 0)

    for j in (1, 3, 2):
        remote(part_out.at[j], part_in.at[j], part_send.at[j], part_recv.at[j], partner).wait_recv()
        remote(lse_out.at[j], lse_in.at[j], lse_send.at[j], lse_recv.at[j], partner).wait_recv()

    best = jnp.maximum(jnp.maximum(top[0], lse_in[1]), jnp.maximum(lse_in[2], lse_in[3]))
    own_ratio = jnp.exp2(top[0] - best)
    ratios = [jnp.exp2(lse_in[j] - best) for j in (1, 2, 3)]
    total = accum[0, HEAD : HEAD + 1, :] * own_ratio + ratios[0] + ratios[1] + ratios[2]
    inverse = 1.0 / total
    own_ratio = own_ratio * inverse
    ratios = [r * inverse for r in ratios]
    for g in range(8):
        cols = slice(g * 128, (g + 1) * 128)
        summed = accum[0, :HEAD, cols] * own_ratio[:, cols]
        for j in (1, 2, 3):
            summed = summed + part_in[j, :, cols].astype(F32) * ratios[j - 1][:, cols]
        turned = summed.astype(BF16).T
        out[:, 2 * g * HEAD : (2 * g + 1) * HEAD] = turned[:64]
        out[:, (2 * g + 1) * HEAD : (2 * g + 2) * HEAD] = turned[64:]

    for slot in (1, 2, 3):
        kv_copy(slot).wait_send()
    for dy in (1, 3, 2):
        q_copy(dy).wait_send()
    for t in range(1, 4):
        for j in range(4):
            hist_copy(t, j).wait_send()
    for j in (1, 3, 2):
        for copy in part_copy(j):
            copy.wait_send()


def attention(table, queries, new_k, new_v, pre_k, pre_v, pool_k, pool_v):
    dma = pltpu.SemaphoreType.DMA
    return pl.pallas_call(
        attention_kernel,
        out_shape=jax.ShapeDtypeStruct((64, 2048), BF16),
        in_specs=[SMEM] + [VMEM] * 7,
        out_specs=VMEM,
        scratch_shapes=[
            pltpu.VMEM((4, ROWS, HEAD), BF16),
            pltpu.VMEM((4, ROWS, 2 * HEAD), BF16),
            pltpu.VMEM((4, 2, 8, 128, 128), BF16),
            pltpu.VMEM((4, 4, 2, 2, 128, 128), BF16),
            pltpu.VMEM((4, 4, 2, 2, 128, 128), BF16),
            pltpu.VMEM((2, 128, 128), BF16),
            pltpu.VMEM((4, 1, ROWS), F32),
            pltpu.VMEM((4, HEAD + ONES, ROWS), F32),
            pltpu.VMEM((UNIT, TILE), F32),
            pltpu.VMEM((UNIT, TILE), F32),
            pltpu.VMEM((4, HEAD, ROWS), BF16),
            pltpu.VMEM((4, HEAD, ROWS), BF16),
            pltpu.VMEM((4, 1, ROWS), F32),
            pltpu.VMEM((4, 1, ROWS), F32),
            dma((4,)),
            dma((4,)),
            dma((4,)),
            dma((4,)),
            dma((4, 4)),
            dma((4, 4)),
            dma((4,)),
            dma((4,)),
            dma((4,)),
            dma((4,)),
        ],
        compiler_params=pltpu.CompilerParams(
            collective_id=0, has_side_effects=True, vmem_limit_bytes=VMEM_LIMIT
        ),
        name="attention",
    )(table, queries, new_k, new_v, pre_k, pre_v, pool_k, pool_v)


def projection_kernel(
    heads,
    weight,
    out,
    gathered,
    sums_out,
    sums_in,
    half_out,
    half_in,
    g_send,
    g_recv,
    relay_send,
    relay_recv,
    z_send,
    z_recv,
    h_send,
    h_recv,
):
    kvh, x, y, core = place()
    z, x_hi = kvh // 2, kvh % 2
    grp = x * 4 + y
    partner = peer(0, 0, 1)

    gathered[0, core] = heads[...]
    greet(
        [partner, peer(1, 0, 0), peer(0, 1, 0), peer(0, 2, 0), peer(0, 3, 0)]
        + [(((z + d) % 4) * 2 + x_hi, grp, core) for d in (1, 2, 3)]
        + [(z * 2 + 1 - x_hi, grp, core)]
    )

    def gather_copy(from_slot, dx, dy):
        slot = (from_slot // 4 + dx) * 4 + (4 - dy) % 4
        return remote(
            gathered.at[from_slot, core],
            gathered.at[slot, core],
            g_send.at[slot],
            g_recv.at[slot],
            peer(dx, dy, 0),
        )

    def relay_copy(slot):
        return remote(
            gathered.at[slot, core],
            gathered.at[slot, core],
            relay_send.at[slot],
            relay_recv.at[slot],
            partner,
        )

    def arrived(slot):
        remote(
            gathered.at[0, core], gathered.at[slot, core], g_send.at[slot], g_recv.at[slot], partner
        ).wait_recv()

    def other_arrived(slot):
        remote(
            gathered.at[slot, core],
            gathered.at[slot, 1 - core],
            relay_send.at[slot],
            relay_recv.at[slot],
            partner,
        ).wait_recv()

    def row_block(slot):
        chip = ((1 - x) if slot // 4 else x) * 4 + (y + slot % 4) % 4
        return chip // 2, chip % 2

    def z_copy(slot):
        to_z, parity = row_block(slot)
        away = (z - to_z + 4) % 4
        return remote(
            sums_out.at[slot],
            sums_in.at[away, parity],
            z_send.at[slot],
            z_recv.at[away, parity],
            (to_z * 2 + x_hi, grp, core),
        )

    def multiply(slot):
        rows = jnp.concatenate([gathered[slot, 0], gathered[slot, 1]], axis=0)

        def columns(n, _):
            at = pl.ds(pl.multiple_of(n * 256, 256), 256)
            sums_out[slot, :, at] = jnp.dot(
                rows, weight[:, at], preferred_element_type=F32
            ).astype(BF16)
            return 0

        lax.fori_loop(0, 4, columns, 0)
        to_z, _ = row_block(slot)

        @pl.when(to_z != z)
        def _():
            z_copy(slot).start()

    relay_copy(0).start()
    gather_copy(0, 1, 0).start()
    for dy in (1, 3, 2):
        gather_copy(0, 0, dy).start()
    other_arrived(0)
    multiply(0)
    order = (4, 1, 3, 2, 5, 7, 6)
    for slot in order:
        arrived(slot)
        relay_copy(slot).start()
        if slot == 4:
            for dy in (1, 3, 2):
                gather_copy(4, 0, dy).start()
        other_arrived(slot)
        multiply(slot)

    def own_slot(parity):
        chip = z * 2 + parity
        return jnp.where(chip // 4 == x, 0, 4) + (chip % 4 - y + 4) % 4

    def summed(parity):
        total = sums_out[own_slot(parity)].astype(F32)
        for away in (1, 2, 3):
            remote(
                sums_out.at[0],
                sums_in.at[away, parity],
                z_send.at[0],
                z_recv.at[away, parity],
                partner,
            ).wait_recv()
        for away in (1, 2, 3):
            total = total + sums_in[away, parity].astype(F32)
        return total

    half_copy = remote(
        half_out, half_in, h_send, h_recv, (z * 2 + 1 - x_hi, grp, core)
    )
    half_out[...] = summed(1 - x_hi).astype(BF16)
    half_copy.start()
    mine = summed(x_hi)
    half_copy.wait_recv()
    out[...] = (mine + half_in[...].astype(F32)).astype(BF16)

    half_copy.wait_send()
    relay_copy(0).wait_send()
    for slot in order:
        relay_copy(slot).wait_send()
    gather_copy(0, 1, 0).wait_send()
    for dy in (1, 3, 2):
        gather_copy(0, 0, dy).wait_send()
        gather_copy(4, 0, dy).wait_send()
    for slot in range(8):
        to_z, _ = row_block(slot)

        @pl.when(to_z != z)
        def _():
            z_copy(slot).wait_send()


def projection(heads, weight):
    dma = pltpu.SemaphoreType.DMA
    return pl.pallas_call(
        projection_kernel,
        out_shape=jax.ShapeDtypeStruct((128, 1024), BF16),
        in_specs=[VMEM] * 2,
        out_specs=VMEM,
        scratch_shapes=[
            pltpu.VMEM((8, 2, 64, 2048), BF16),
            pltpu.VMEM((8, 128, 1024), BF16),
            pltpu.VMEM((4, 2, 128, 1024), BF16),
            pltpu.VMEM((128, 1024), BF16),
            pltpu.VMEM((128, 1024), BF16),
            dma((8,)),
            dma((8,)),
            dma((8,)),
            dma((8,)),
            dma((8,)),
            dma((4, 2)),
            dma,
            dma,
        ],
        compiler_params=pltpu.CompilerParams(
            collective_id=1, has_side_effects=True, vmem_limit_bytes=VMEM_LIMIT
        ),
        name="projection",
    )(heads, weight)


def block_table(hist_blocks, hist_len):
    owners = pairs = 16
    ids = hist_blocks.reshape(pairs, 32)
    position = jnp.arange(32, dtype=jnp.int32)
    lengths = jnp.repeat(hist_len.reshape(pairs, 2), 16, axis=1)
    live = jnp.clip(lengths - 128 * (position % 16)[None, :], 0, 128)
    code = position[None, :] * 16384 + live * 64 + (position // 16)[None, :] * 32 + ids % 32
    named = (ids // 32)[None] == jnp.arange(owners, dtype=jnp.int32)[:, None, None]
    first = jnp.min(jnp.where(named, code[None], 2**30), axis=2)
    second = jnp.max(jnp.where(named, code[None], -1), axis=2)
    return jnp.concatenate([first.reshape(-1), second.reshape(-1)])


def on_device(
    queries,
    new_keys,
    new_values,
    prefix_keys,
    prefix_values,
    pool_keys,
    pool_values,
    hist_blocks,
    hist_len,
    out_weight,
):
    table = block_table(hist_blocks, hist_len)
    heads = attention(
        table,
        queries.reshape(64, 2048),
        new_keys.reshape(64, HEAD),
        new_values.reshape(64, HEAD),
        prefix_keys,
        prefix_values,
        pool_keys,
        pool_values,
    )
    projected = projection(heads, out_weight)
    return heads.reshape(2, 32, 2048), projected.reshape(4, 32, 1024)


def solution(mesh):
    in_specs = (
        P(("grp", "blk"), None, "kvh"),
        P(("grp", "blk"), None, "kvh"),
        P(("grp", "blk"), None, "kvh"),
        P(("grp", "blk"), "kvh"),
        P(("grp", "blk"), "kvh"),
        P(("grp", "blk"), None, "kvh"),
        P(("grp", "blk"), None, "kvh"),
        P(),
        P(),
        P("kvh", ("grp", "blk")),
    )
    out_specs = (P(("grp", "blk"), None, "kvh"), P("kvh", None, ("grp", "blk")))
    return jax.shard_map(
        on_device, mesh=mesh, in_specs=in_specs, out_specs=out_specs, check_vma=False
    )
```

```python
import functools
import math

import jax
import jax.numpy as jnp
from jax import lax
from jax.experimental import pallas as pl
from jax.experimental.pallas import tpu as pltpu
from jax.sharding import PartitionSpec as P

F32 = jnp.float32
BF16 = jnp.bfloat16
HEAD = 128
ROWS = 1024
TILE = 512
UNIT = 1024
ONES = 16
LOG2_SCALE = HEAD**-0.5 * math.log2(math.e)
HIDDEN = -1e30
NT = (((1,), (1,)), ((), ()))
Z_COLS = 512
X_COLS = 1024 - Z_COLS
VMEM_LIMIT = 60 * 2**20
VMEM = pl.BlockSpec(memory_space=pltpu.VMEM)
SMEM = pl.BlockSpec(memory_space=pltpu.SMEM)


def place():
    kvh, grp, core = lax.axis_index("kvh"), lax.axis_index("grp"), lax.axis_index("blk")
    return kvh, grp // 4, grp % 4, core


def peer(dx, dy, dc):
    kvh, x, y, core = place()
    px = 1 - x if dx else x
    pc = 1 - core if dc else core
    return (kvh, px * 4 + (y + dy) % 4, pc)


def remote(src, dst, send, recv, to):
    return pltpu.make_async_remote_copy(
        src_ref=src,
        dst_ref=dst,
        send_sem=send,
        recv_sem=recv,
        device_id=to,
        device_id_type=pl.DeviceIdType.MESH,
    )


def greet(peers):
    barrier = pltpu.get_barrier_semaphore()
    for to in peers:
        pl.semaphore_signal(barrier, inc=1, device_id=to, device_id_type=pl.DeviceIdType.MESH)
    pl.semaphore_wait(barrier, len(peers))


def turn(i):
    return jnp.where(i == 3, 0, 1 + (2 * i) % 3)


def layer_kernel(
    table,
    q_in,
    new_k,
    new_v,
    pre_k,
    pre_v,
    pool_k,
    pool_v,
    weight_in,
    heads,
    out_z,
    out_x,
    half_in,
    q_raw,
    q_two,
    kv,
    hist_out,
    hist,
    new_kv,
    top,
    accum,
    score_a,
    score_b,
    part_out,
    part_in,
    lse_out,
    lse_in,
    q_send,
    q_recv,
    kv_send,
    kv_recv,
    hist_send,
    hist_recv,
    part_send,
    part_recv,
    lse_send,
    lse_recv,
    weight,
    gathered,
    sums_z,
    sums_x,
    z_in,
    pair_in,
    merged,
    merged_in,
    half_out,
    w_sem,
    g_send,
    g_recv,
    relay_send,
    relay_recv,
    z_send,
    z_recv,
    pair_send,
    pair_recv,
    m_send,
    m_recv,
    h_send,
    h_recv,
):
    kvh, x, y, core = place()
    z, x_hi = kvh // 2, kvh % 2
    grp = x * 4 + y
    partner = peer(0, 0, 1)
    across = (z * 2 + 1 - x_hi, grp, core)
    weight_copy = pltpu.make_async_copy(weight_in, weight, w_sem)
    weight_copy.start()
    scores = (score_a, score_b)

    def holder(t):
        dx, dc = t // 2, t % 2
        return ((1 - x if dx else x) * 4 + y) * 2 + (1 - core if dc else core)

    def entry(first_or_second, owner, request_pair):
        return table[first_or_second * 256 + owner * 16 + request_pair]

    def score(j, keys, tile, mask):
        count = keys.shape[0]
        value = lax.dot_general(
            jnp.concatenate([keys, keys], axis=1),
            q_two[j, tile * TILE : (tile + 1) * TILE, :],
            NT,
            preferred_element_type=F32,
        )
        if mask is None:
            scores[tile][:count] = value
        else:
            for b in range(count // 128):
                rows = slice(b * 128, (b + 1) * 128)
                scores[tile][rows] = jnp.where(mask(b, tile), value[rows], HIDDEN)

    def weigh(j, values, tile, count):
        cols = slice(tile * TILE, (tile + 1) * TILE)
        old = top[j, :, cols]
        newest = jnp.maximum(old, scores[tile][:count].max(axis=0, keepdims=True))
        shrink = jnp.exp2(old - newest)
        top[j, :, cols] = newest
        weights = jnp.exp2(scores[tile][:count] - newest).astype(BF16)
        values = jnp.concatenate([values, jnp.ones((ONES, count), BF16)], axis=0)
        accum[j, :, cols] = accum[j, :, cols] * shrink + jnp.dot(
            values, weights, preferred_element_type=F32
        )

    def absorb(j, parts):
        tasks = [(part, tile) for part in parts for tile in range(2)]
        score(j, tasks[0][0][0](), tasks[0][1], tasks[0][0][2])
        for at, ((keys, values, mask), tile) in enumerate(tasks):
            if at + 1 < len(tasks):
                (after_keys, _, after_mask), after_tile = tasks[at + 1]
                score(j, after_keys(), after_tile, after_mask)
            loaded = values()
            weigh(j, loaded, tile, loaded.shape[1])

    def prefix_part(slot):
        return (
            lambda: jnp.concatenate([kv[slot, 0, b] for b in range(8)], axis=0),
            lambda: jnp.concatenate([kv[slot, 1, b] for b in range(8)], axis=1),
            None,
        )

    def hist_part(j):
        request_pair = (x * 4 + (y + j) % 4) * 2 + core

        def mask(b, tile):
            code = entry(b % 2, holder(b // 2), request_pair)
            lane = lax.broadcasted_iota(jnp.int32, (1, TILE), 1)
            limit = jnp.where((lane // 32) % 2 == (code // 32) % 2, (code // 64) % 256, 0)
            return lax.broadcasted_iota(jnp.int32, (128, TILE), 0) < limit

        return (
            lambda: jnp.concatenate(
                [hist[t, j, 0, i] for t in range(4) for i in range(2)], axis=0
            ),
            lambda: jnp.concatenate(
                [hist[t, j, 1, i] for t in range(4) for i in range(2)], axis=1
            ),
            mask,
        )

    def new_part():
        def mask(b, tile):
            lane = lax.broadcasted_iota(jnp.int32, (128, TILE), 1) % 64
            key = lax.broadcasted_iota(jnp.int32, (128, TILE), 0)
            return (key <= lane) & (key >= (lane // 32) * 32)

        return (lambda: new_kv[0], lambda: new_kv[1], mask)

    def start_state(j):
        q = q_raw[j].astype(F32) * LOG2_SCALE
        high = q.astype(BF16)
        q_two[j, :, :HEAD] = high
        q_two[j, :, HEAD:] = (q - high.astype(F32)).astype(BF16)
        top[j] = jnp.full((1, ROWS), HIDDEN, F32)
        accum[j] = jnp.zeros((HEAD + ONES, ROWS), F32)

    for g in range(16):
        q_raw[0, g * 64 : (g + 1) * 64, :] = q_in[:, g * HEAD : (g + 1) * HEAD]
    for b in range(8):
        kv[0, 0, b] = pre_k[b * 128 : (b + 1) * 128, :]
        kv[0, 1, b] = pre_v[b * 128 : (b + 1) * 128, :].T

    greet(
        [partner, peer(1, 0, 0), peer(1, 0, 1), peer(0, 1, 0), peer(0, 2, 0), peer(0, 3, 0), across]
        + [(((z + d) % 4) * 2 + x_hi, grp, core) for d in (1, 2, 3)]
    )

    def kv_copy(slot):
        src, to = ((0, partner), (0, peer(1, 0, 0)), (2, partner))[slot - 1]
        return remote(kv.at[src], kv.at[slot], kv_send.at[slot], kv_recv.at[slot], to)

    def q_copy(dy):
        to = peer(0, dy, 0)
        slot = (4 - dy) % 4
        return remote(q_raw.at[0], q_raw.at[slot], q_send.at[slot], q_recv.at[slot], to)

    def hist_copy(t, j):
        return remote(
            hist_out.at[t, j],
            hist.at[t, j],
            hist_send.at[t, j],
            hist_recv.at[t, j],
            peer(t // 2, 0, t % 2),
        )

    def part_copy(j):
        slot = (4 - j) % 4
        to = peer(0, j, 0)
        return (
            remote(part_out.at[j], part_in.at[slot], part_send.at[j], part_recv.at[slot], to),
            remote(lse_out.at[j], lse_in.at[slot], lse_send.at[j], lse_recv.at[slot], to),
        )

    kv_copy(2).start()
    kv_copy(1).start()
    for dy in (1, 3, 2):
        q_copy(dy).start()

    def fill(i, _):
        j = turn(i)
        for t in range(4):
            request_pair = (
                ((1 - x if t // 2 else x) * 4 + (y + j) % 4) * 2 + (1 - core if t % 2 else core)
            )
            own = (x * 4 + y) * 2 + core
            store = hist if t == 0 else hist_out
            for n in range(2):
                local = entry(n, own, request_pair) % 32
                store[t, j, 0, n] = pool_k[local]
                store[t, j, 1, n] = pool_v[local].T
            if t > 0:
                hist_copy(t, j).start()
        return 0

    lax.fori_loop(0, 4, fill, 0)

    start_state(0)
    new_kv[...] = jnp.zeros((2, 128, 128), BF16)
    new_kv[0, :64, :] = new_k[...]
    new_kv[1, :, :] = jnp.concatenate([new_v[...], jnp.zeros((64, HEAD), BF16)], axis=0).T
    absorb(0, [prefix_part(0), new_part()])
    kv_copy(1).wait_recv()
    absorb(0, [prefix_part(1)])

    def near(i, _):
        @pl.when(i == 2)
        def _():
            kv_copy(2).wait_recv()
            kv_copy(3).start()

        j = turn(i)
        remote(q_raw.at[0], q_raw.at[j], q_send.at[j], q_recv.at[j], partner).wait_recv()
        start_state(j)
        absorb(j, [prefix_part(0), prefix_part(1)])
        return 0

    lax.fori_loop(0, 3, near, 0)
    kv_copy(3).wait_recv()

    def far(i, _):
        j = turn(i)
        absorb(j, [prefix_part(2), prefix_part(3)])
        for t in range(1, 4):
            hist_copy(t, j).wait_recv()
        absorb(j, [hist_part(j)])

        @pl.when(i < 3)
        def _():
            total = accum[j, HEAD : HEAD + 1, :]
            part_out[j] = (accum[j, :HEAD, :] / total).astype(BF16)
            lse_out[j] = top[j] + jnp.log2(total)
            for copy in part_copy(j):
                copy.start()

        return 0

    lax.fori_loop(0, 4, far, 0)

    for j in (1, 3, 2):
        remote(part_out.at[j], part_in.at[j], part_send.at[j], part_recv.at[j], partner).wait_recv()
        remote(lse_out.at[j], lse_in.at[j], lse_send.at[j], lse_recv.at[j], partner).wait_recv()

    best = jnp.maximum(jnp.maximum(top[0], lse_in[1]), jnp.maximum(lse_in[2], lse_in[3]))
    own_ratio = jnp.exp2(top[0] - best)
    ratios = [jnp.exp2(lse_in[j] - best) for j in (1, 2, 3)]
    total = accum[0, HEAD : HEAD + 1, :] * own_ratio + ratios[0] + ratios[1] + ratios[2]
    inverse = 1.0 / total
    own_ratio = own_ratio * inverse
    ratios = [r * inverse for r in ratios]
    for g in range(8):
        cols = slice(g * 128, (g + 1) * 128)
        summed = accum[0, :HEAD, cols] * own_ratio[:, cols]
        for j in (1, 2, 3):
            summed = summed + part_in[j, :, cols].astype(F32) * ratios[j - 1][:, cols]
        turned = summed.astype(BF16).T
        for n in range(2):
            here = slice((2 * g + n) * HEAD, (2 * g + n + 1) * HEAD)
            heads[:, here] = turned[n * 64 : (n + 1) * 64]
            gathered[0, core, :, here] = turned[n * 64 : (n + 1) * 64]

    def gather_copy(from_slot, dx, dy):
        slot = (from_slot // 4 + dx) * 4 + (from_slot % 4 + 4 - dy) % 4
        return remote(
            gathered.at[from_slot, core],
            gathered.at[slot, core],
            g_send.at[slot],
            g_recv.at[slot],
            peer(dx, dy, 0),
        )

    def onward(column):
        from_slot = column * 4 + 3 - 2 * core
        slot = column * 4 + 2
        return remote(
            gathered.at[from_slot, core],
            gathered.at[slot, core],
            g_send.at[slot],
            g_recv.at[slot],
            peer(0, 1 + 2 * core, 0),
        )

    def relay_copy(slot):
        return remote(
            gathered.at[slot, core],
            gathered.at[slot, core],
            relay_send.at[slot],
            relay_recv.at[slot],
            partner,
        )

    def arrived(slot):
        remote(
            gathered.at[0, core], gathered.at[slot, core], g_send.at[slot], g_recv.at[slot], partner
        ).wait_recv()
        relay_copy(slot).start()

    def row_block(slot):
        chip = (x + slot // 4) % 2 * 4 + (y + slot % 4) % 4
        return chip // 2, chip % 2

    def z_copy(slot):
        to_z, parity = row_block(slot)
        away = (z - to_z + 4) % 4
        return remote(
            sums_z.at[slot],
            z_in.at[away, parity],
            z_send.at[slot],
            z_recv.at[away, parity],
            (to_z * 2 + x_hi, grp, core),
        )

    def pair_copy(slot):
        return remote(
            sums_x.at[slot], pair_in.at[slot], pair_send.at[slot], pair_recv.at[slot], across
        )

    def multiply(slot):
        remote(
            gathered.at[slot, core],
            gathered.at[slot, 1 - core],
            relay_send.at[slot],
            relay_recv.at[slot],
            partner,
        ).wait_recv()
        rows = jnp.concatenate([gathered[slot, 0], gathered[slot, 1]], axis=0)
        to_z, parity = row_block(slot)

        for part, (sums, start) in enumerate(((sums_x, Z_COLS), (sums_z, 0))):

            def columns(n, _, sums=sums, start=start):
                at = pl.ds(pl.multiple_of(n * 256, 256), 256)
                from_weight = pl.ds(pl.multiple_of(start + n * 256, 256), 256)
                sums[slot, :, at] = jnp.dot(
                    rows, weight[:, from_weight], preferred_element_type=F32
                ).astype(BF16)
                return 0

            lax.fori_loop(0, sums.shape[2] // 256, columns, 0)
            if part == 0:

                @pl.when(parity != x_hi)
                def _():
                    pair_copy(slot).start()

            else:

                @pl.when(to_z != z)
                def _():
                    z_copy(slot).start()

    def merge_slot(i):
        other = (y + x_hi) % 2
        return (1 - other) * ((i % 2) * 4 + (i // 2) * 2) + other * (2 * i + 1)

    def merged_copy(slot):
        to_z, _ = row_block(slot)
        return remote(
            merged.at[slot],
            merged_in.at[(z - to_z + 4) % 4],
            m_send.at[slot],
            m_recv.at[(z - to_z + 4) % 4],
            (to_z * 2 + x_hi, grp, core),
        )

    def merge(i):
        slot = merge_slot(i)
        remote(
            sums_x.at[slot], pair_in.at[slot], pair_send.at[slot], pair_recv.at[slot], across
        ).wait_recv()
        merged[slot] = (sums_x[slot].astype(F32) + pair_in[slot].astype(F32)).astype(BF16)
        to_z, _ = row_block(slot)

        @pl.when(to_z != z)
        def _():
            merged_copy(slot).start()

    relay_copy(0).start()
    for dx, dy in ((1, 0), (0, 1), (0, 3)):
        gather_copy(0, dx, dy).start()
    weight_copy.wait()
    multiply(0)
    arrived(4)
    gather_copy(4, 0, 1).start()
    gather_copy(4, 0, 3).start()
    arrived(1)
    arrived(3)
    onward(0).start()
    multiply(4)
    multiply(1)
    multiply(3)
    arrived(5)
    arrived(7)
    onward(1).start()
    merge(0)
    multiply(5)
    merge(1)
    multiply(7)
    arrived(2)
    multiply(2)
    arrived(6)
    multiply(6)
    merge(2)
    merge(3)

    def own_slot(parity):
        chip = z * 2 + parity
        return (chip // 4 + x) % 2 * 4 + (chip % 4 - y + 4) % 4

    def z_total(parity):
        for away in (1, 2, 3):
            remote(
                sums_z.at[0], z_in.at[away, parity], z_send.at[0], z_recv.at[away, parity], partner
            ).wait_recv()
        total = sums_z[own_slot(parity)].astype(F32)
        for away in (1, 2, 3):
            total = total + z_in[away, parity].astype(F32)
        return total.astype(BF16)

    half_copy = remote(half_out, half_in, h_send, h_recv, across)
    half_out[...] = z_total(1 - x_hi)
    half_copy.start()
    out_z[...] = z_total(x_hi)
    for away in (1, 2, 3):
        remote(
            merged.at[0], merged_in.at[away], m_send.at[0], m_recv.at[away], partner
        ).wait_recv()
    total = merged[own_slot(x_hi)].astype(F32)
    for away in (1, 2, 3):
        total = total + merged_in[away].astype(F32)
    out_x[...] = total.astype(BF16)
    half_copy.wait_recv()

    half_copy.wait_send()
    for slot in range(8):
        relay_copy(slot).wait_send()
        to_z, parity = row_block(slot)

        @pl.when(to_z != z)
        def _():
            z_copy(slot).wait_send()

        @pl.when(parity != x_hi)
        def _():
            pair_copy(slot).wait_send()

        @pl.when((parity == x_hi) & (to_z != z))
        def _():
            merged_copy(slot).wait_send()

    for dx, dy in ((1, 0), (0, 1), (0, 3)):
        gather_copy(0, dx, dy).wait_send()
    for dy in (1, 3):
        gather_copy(4, 0, dy).wait_send()
    onward(0).wait_send()
    onward(1).wait_send()
    for slot in (1, 2, 3):
        kv_copy(slot).wait_send()
    for dy in (1, 3, 2):
        q_copy(dy).wait_send()
    for t in range(1, 4):
        for j in range(4):
            hist_copy(t, j).wait_send()
    for j in (1, 3, 2):
        for copy in part_copy(j):
            copy.wait_send()


def layer(table, queries, new_k, new_v, pre_k, pre_v, pool_k, pool_v, weight):
    dma = pltpu.SemaphoreType.DMA
    return pl.pallas_call(
        layer_kernel,
        out_shape=[
            jax.ShapeDtypeStruct((64, 2048), BF16),
            jax.ShapeDtypeStruct((128, Z_COLS), BF16),
            jax.ShapeDtypeStruct((128, X_COLS), BF16),
            jax.ShapeDtypeStruct((128, Z_COLS), BF16),
        ],
        in_specs=[SMEM] + [VMEM] * 7 + [pl.BlockSpec(memory_space=pl.ANY)],
        out_specs=[VMEM] * 4,
        scratch_shapes=[
            pltpu.VMEM((4, ROWS, HEAD), BF16),
            pltpu.VMEM((4, ROWS, 2 * HEAD), BF16),
            pltpu.VMEM((4, 2, 8, 128, 128), BF16),
            pltpu.VMEM((4, 4, 2, 2, 128, 128), BF16),
            pltpu.VMEM((4, 4, 2, 2, 128, 128), BF16),
            pltpu.VMEM((2, 128, 128), BF16),
            pltpu.VMEM((4, 1, ROWS), F32),
            pltpu.VMEM((4, HEAD + ONES, ROWS), F32),
            pltpu.VMEM((UNIT, TILE), F32),
            pltpu.VMEM((UNIT, TILE), F32),
            pltpu.VMEM((4, HEAD, ROWS), BF16),
            pltpu.VMEM((4, HEAD, ROWS), BF16),
            pltpu.VMEM((4, 1, ROWS), F32),
            pltpu.VMEM((4, 1, ROWS), F32),
            dma((4,)),
            dma((4,)),
            dma((4,)),
            dma((4,)),
            dma((4, 4)),
            dma((4, 4)),
            dma((4,)),
            dma((4,)),
            dma((4,)),
            dma((4,)),
            pltpu.VMEM((2048, 1024), BF16),
            pltpu.VMEM((8, 2, 64, 2048), BF16),
            pltpu.VMEM((8, 128, Z_COLS), BF16),
            pltpu.VMEM((8, 128, X_COLS), BF16),
            pltpu.VMEM((4, 2, 128, Z_COLS), BF16),
            pltpu.VMEM((8, 128, X_COLS), BF16),
            pltpu.VMEM((8, 128, X_COLS), BF16),
            pltpu.VMEM((4, 128, X_COLS), BF16),
            pltpu.VMEM((128, Z_COLS), BF16),
            dma,
            dma((8,)),
            dma((8,)),
            dma((8,)),
            dma((8,)),
            dma((8,)),
            dma((4, 2)),
            dma((8,)),
            dma((8,)),
            dma((8,)),
            dma((4,)),
            dma,
            dma,
        ],
        compiler_params=pltpu.CompilerParams(
            collective_id=0, has_side_effects=True, vmem_limit_bytes=VMEM_LIMIT
        ),
        name="layer",
    )(table, queries, new_k, new_v, pre_k, pre_v, pool_k, pool_v, weight)


def block_table(hist_blocks, hist_len):
    owners = pairs = 16
    ids = hist_blocks.reshape(pairs, 32)
    position = jnp.arange(32, dtype=jnp.int32)
    lengths = jnp.repeat(hist_len.reshape(pairs, 2), 16, axis=1)
    live = jnp.clip(lengths - 128 * (position % 16)[None, :], 0, 128)
    code = position[None, :] * 16384 + live * 64 + (position // 16)[None, :] * 32 + ids % 32
    named = (ids // 32)[None] == jnp.arange(owners, dtype=jnp.int32)[:, None, None]
    first = jnp.min(jnp.where(named, code[None], 2**30), axis=2)
    second = jnp.max(jnp.where(named, code[None], -1), axis=2)
    return jnp.concatenate([first.reshape(-1), second.reshape(-1)])


def on_device(
    queries,
    new_keys,
    new_values,
    prefix_keys,
    prefix_values,
    pool_keys,
    pool_values,
    hist_blocks,
    hist_len,
    out_weight,
):
    table = block_table(hist_blocks, hist_len)
    heads, out_z, out_x, half = layer(
        table,
        queries.reshape(64, 2048),
        new_keys.reshape(64, HEAD),
        new_values.reshape(64, HEAD),
        prefix_keys,
        prefix_values,
        pool_keys,
        pool_values,
        out_weight,
    )
    out_z = (out_z.astype(F32) + half.astype(F32)).astype(BF16)
    projected = jnp.concatenate([out_z, out_x], axis=1)
    return heads.reshape(2, 32, 2048), projected.reshape(4, 32, 1024)


def solution(mesh):
    in_specs = (
        P(("grp", "blk"), None, "kvh"),
        P(("grp", "blk"), None, "kvh"),
        P(("grp", "blk"), None, "kvh"),
        P(("grp", "blk"), "kvh"),
        P(("grp", "blk"), "kvh"),
        P(("grp", "blk"), None, "kvh"),
        P(("grp", "blk"), None, "kvh"),
        P(),
        P(),
        P("kvh", ("grp", "blk")),
    )
    out_specs = (P(("grp", "blk"), None, "kvh"), P("kvh", None, ("grp", "blk")))
    return jax.shard_map(
        on_device, mesh=mesh, in_specs=in_specs, out_specs=out_specs, check_vma=False
    )
```

```python
import functools
import math

import jax
import jax.numpy as jnp
from jax import lax
from jax.experimental import pallas as pl
from jax.experimental.pallas import tpu as pltpu
from jax.sharding import PartitionSpec as P

F32 = jnp.float32
BF16 = jnp.bfloat16
HEAD = 128
ROWS = 1024
TILE = 512
UNIT = 1024
ONES = 16
LOG2_SCALE = HEAD**-0.5 * math.log2(math.e)
HIDDEN = -1e30
NT = (((1,), (1,)), ((), ()))
Z_COLS = 512
X_COLS = 1024 - Z_COLS
VMEM_LIMIT = 60 * 2**20
VMEM = pl.BlockSpec(memory_space=pltpu.VMEM)


def place():
    kvh, grp, core = lax.axis_index("kvh"), lax.axis_index("grp"), lax.axis_index("blk")
    return kvh, grp // 4, grp % 4, core


def peer(dx, dy, dc):
    kvh, x, y, core = place()
    px = 1 - x if dx else x
    pc = 1 - core if dc else core
    return (kvh, px * 4 + (y + dy) % 4, pc)


def remote(src, dst, send, recv, to):
    return pltpu.make_async_remote_copy(
        src_ref=src,
        dst_ref=dst,
        send_sem=send,
        recv_sem=recv,
        device_id=to,
        device_id_type=pl.DeviceIdType.MESH,
    )


def turn(i):
    return jnp.where(i == 3, 0, 1 + (2 * i) % 3)


def layer_kernel(
    blocks,
    lengths,
    new_k,
    new_v,
    q_hbm,
    pre_k,
    pre_v,
    pool_k_hbm,
    pool_v_hbm,
    weight_in,
    heads,
    out,
    half_in,
    q_in,
    v_in,
    pool_k,
    pool_v,
    table_wide,
    table,
    in_sem,
    q_raw,
    q_two,
    kv,
    hist_out,
    hist,
    new_kv,
    top,
    accum,
    score_a,
    score_b,
    part_out,
    part_in,
    lse_out,
    lse_in,
    q_send,
    q_recv,
    kv_send,
    kv_recv,
    hist_send,
    hist_recv,
    part_send,
    part_recv,
    lse_send,
    lse_recv,
    weight,
    gathered,
    sums_z,
    sums_x,
    z_in,
    pair_in,
    merged,
    merged_in,
    half_out,
    w_sem,
    g_send,
    g_recv,
    relay_send,
    relay_recv,
    z_send,
    z_recv,
    pair_send,
    pair_recv,
    m_send,
    m_recv,
    h_send,
    h_recv,
):
    kvh, x, y, core = place()
    z, x_hi = kvh // 2, kvh % 2
    grp = x * 4 + y
    partner = peer(0, 0, 1)
    across = (z * 2 + 1 - x_hi, grp, core)
    weight_copy = pltpu.make_async_copy(weight_in, weight, w_sem)
    inputs = [
        pltpu.make_async_copy(src, dst, in_sem.at[n])
        for n, (src, dst) in enumerate(
            (
                (pre_k, kv.at[0, 0]),
                (pre_v, v_in),
                (q_hbm, q_in),
                (pool_k_hbm, pool_k),
                (pool_v_hbm, pool_v),
            )
        )
    ]
    for copy in inputs:
        copy.start()
    weight_copy.start()
    barrier = pltpu.get_barrier_semaphore()
    peers = [partner, peer(1, 0, 0), peer(1, 0, 1), peer(0, 1, 0), peer(0, 2, 0), peer(0, 3, 0), across]
    peers += [(((z + d) % 4) * 2 + x_hi, grp, core) for d in (1, 2, 3)]
    for to in peers:
        pl.semaphore_signal(barrier, inc=1, device_id=to, device_id_type=pl.DeviceIdType.MESH)
    scores = (score_a, score_b)

    def holder(t):
        dx, dc = t // 2, t % 2
        return ((1 - x if dx else x) * 4 + y) * 2 + (1 - core if dc else core)

    def fill_table():
        ids = blocks[...]
        request = lax.broadcasted_iota(jnp.int32, ids.shape, 1)
        block = lax.broadcasted_iota(jnp.int32, ids.shape, 0)
        live = jnp.clip(lengths[...] - 128 * block, 0, 128)
        code = ((request & 1) * 16 + block) * 16384 + live * 64 + (request & 1) * 32 + (ids & 31)
        for t in range(4):
            named = (ids >> 5) == holder(t)
            table_wide[2 * t : 2 * t + 1, :32] = jnp.min(
                jnp.where(named, code, 2**30), axis=0, keepdims=True
            )
            table_wide[2 * t + 1 : 2 * t + 2, :32] = jnp.max(
                jnp.where(named, code, -1), axis=0, keepdims=True
            )

    def entry(n, t, request_pair):
        one = table[2 * t + n, 2 * request_pair]
        two = table[2 * t + n, 2 * request_pair + 1]
        return jnp.maximum(one, two) if n else jnp.minimum(one, two)

    def score(j, keys, tile, mask):
        count = keys.shape[0]
        value = lax.dot_general(
            jnp.concatenate([keys, keys], axis=1),
            q_two[j, tile * TILE : (tile + 1) * TILE, :],
            NT,
            preferred_element_type=F32,
        )
        if mask is None:
            scores[tile][:count] = value
        else:
            for b in range(count // 128):
                rows = slice(b * 128, (b + 1) * 128)
                scores[tile][rows] = jnp.where(mask(b, tile), value[rows], HIDDEN)

    def weigh(j, values, tile, count):
        cols = slice(tile * TILE, (tile + 1) * TILE)
        old = top[j, :, cols]
        newest = jnp.maximum(old, scores[tile][:count].max(axis=0, keepdims=True))
        shrink = jnp.exp2(old - newest)
        top[j, :, cols] = newest
        weights = jnp.exp2(scores[tile][:count] - newest).astype(BF16)
        values = jnp.concatenate([values, jnp.ones((ONES, count), BF16)], axis=0)
        accum[j, :, cols] = accum[j, :, cols] * shrink + jnp.dot(
            values, weights, preferred_element_type=F32
        )

    def absorb(j, parts):
        tasks = [(part, tile) for part in parts for tile in range(2)]
        score(j, tasks[0][0][0](), tasks[0][1], tasks[0][0][2])
        for at, ((keys, values, mask), tile) in enumerate(tasks):
            if at + 1 < len(tasks):
                (after_keys, _, after_mask), after_tile = tasks[at + 1]
                score(j, after_keys(), after_tile, after_mask)
            loaded = values()
            weigh(j, loaded, tile, loaded.shape[1])

    def prefix_part(slot):
        return (
            lambda: jnp.concatenate([kv[slot, 0, b] for b in range(8)], axis=0),
            lambda: jnp.concatenate([kv[slot, 1, b] for b in range(8)], axis=1),
            None,
        )

    def hist_part(j):
        request_pair = (x * 4 + (y + j) % 4) * 2 + core

        def mask(b, tile):
            code = entry(b % 2, b // 2, request_pair)
            lane = lax.broadcasted_iota(jnp.int32, (1, TILE), 1)
            limit = jnp.where((lane // 32) % 2 == (code // 32) % 2, (code // 64) % 256, 0)
            return lax.broadcasted_iota(jnp.int32, (128, TILE), 0) < limit

        return (
            lambda: jnp.concatenate(
                [hist[t, j, 0, i] for t in range(4) for i in range(2)], axis=0
            ),
            lambda: jnp.concatenate(
                [hist[t, j, 1, i] for t in range(4) for i in range(2)], axis=1
            ),
            mask,
        )

    def new_part():
        def mask(b, tile):
            lane = lax.broadcasted_iota(jnp.int32, (128, TILE), 1) % 64
            key = lax.broadcasted_iota(jnp.int32, (128, TILE), 0)
            return (key <= lane) & (key >= (lane // 32) * 32)

        return (lambda: new_kv[0], lambda: new_kv[1], mask)

    def start_state(j):
        q = q_raw[j].astype(F32) * LOG2_SCALE
        high = q.astype(BF16)
        q_two[j, :, :HEAD] = high
        q_two[j, :, HEAD:] = (q - high.astype(F32)).astype(BF16)
        top[j] = jnp.full((1, ROWS), HIDDEN, F32)
        accum[j] = jnp.zeros((HEAD + ONES, ROWS), F32)

    fill_table()
    table_copy = pltpu.make_async_copy(table_wide, table, in_sem.at[5])
    table_copy.start()
    for copy in inputs[:3]:
        copy.wait()
    for b in range(8):
        kv[0, 1, b] = v_in[b].T
    for g in range(16):
        q_raw[0, g * 64 : (g + 1) * 64, :] = q_in[:, g * HEAD : (g + 1) * HEAD]
    pl.semaphore_wait(barrier, len(peers))

    def kv_copy(slot):
        src, to = ((0, partner), (0, peer(1, 0, 0)), (2, partner))[slot - 1]
        return remote(kv.at[src], kv.at[slot], kv_send.at[slot], kv_recv.at[slot], to)

    def q_copy(dy):
        to = peer(0, dy, 0)
        slot = (4 - dy) % 4
        return remote(q_raw.at[0], q_raw.at[slot], q_send.at[slot], q_recv.at[slot], to)

    def hist_copy(t, j):
        return remote(
            hist_out.at[t, j],
            hist.at[t, j],
            hist_send.at[t, j],
            hist_recv.at[t, j],
            (kvh, (x + t // 2) % 2 * 4 + y, (core + t % 2) % 2),
        )

    def part_copy(j):
        slot = (4 - j) % 4
        to = peer(0, j, 0)
        return (
            remote(part_out.at[j], part_in.at[slot], part_send.at[j], part_recv.at[slot], to),
            remote(lse_out.at[j], lse_in.at[slot], lse_send.at[j], lse_recv.at[slot], to),
        )

    kv_copy(2).start()
    kv_copy(1).start()
    for dy in (1, 3, 2):
        q_copy(dy).start()

    def gather_blocks(t, j, store):
        request_pair = ((x + t // 2) % 2 * 4 + (y + j) % 4) * 2 + (core + t % 2) % 2
        for n in range(2):
            local = entry(n, 0, request_pair) & 31
            store[t, j, 0, n] = pool_k[local]
            store[t, j, 1, n] = pool_v[local].T

    def send_along_x(lane):
        def fill(i, _):
            t, j = 2 + (core + lane) % 2, turn(i)
            gather_blocks(t, j, hist_out)
            hist_copy(t, j).start()
            return 0

        lax.fori_loop(0, 4, fill, 0)

    def send_near(i, _):
        j = turn(i)
        gather_blocks(1, j, hist_out)
        hist_copy(1, j).start()
        gather_blocks(0, j, hist)
        return 0

    for copy in inputs[3:]:
        copy.wait()
    table_copy.wait()
    send_along_x(0)
    send_along_x(1)
    lax.fori_loop(0, 4, send_near, 0)

    start_state(0)
    new_kv[...] = jnp.zeros((2, 128, 128), BF16)
    new_kv[0, :64, :] = new_k[...]
    new_kv[1, :, :] = jnp.concatenate([new_v[...], jnp.zeros((64, HEAD), BF16)], axis=0).T
    absorb(0, [prefix_part(0), new_part()])
    kv_copy(1).wait_recv()
    absorb(0, [prefix_part(1)])

    def near(i, _):
        @pl.when(i == 2)
        def _():
            kv_copy(2).wait_recv()
            kv_copy(3).start()

        j = turn(i)
        remote(q_raw.at[0], q_raw.at[j], q_send.at[j], q_recv.at[j], partner).wait_recv()
        start_state(j)
        absorb(j, [prefix_part(0), prefix_part(1)])
        return 0

    lax.fori_loop(0, 3, near, 0)
    kv_copy(3).wait_recv()

    def far(i, _):
        is_far = jnp.where(core == 0, 1 - i % 2, 1 - i // 4) == 1
        order = jnp.where(core == 0, i // 2, i % 4)
        j = turn(order)

        @pl.when(is_far)
        def _():
            absorb(j, [prefix_part(2), prefix_part(3)])

        @pl.when(jnp.logical_not(is_far))
        def _():
            for t in range(1, 4):
                hist_copy(t, j).wait_recv()
            absorb(j, [hist_part(j)])

            @pl.when(order < 3)
            def _():
                total = accum[j, HEAD : HEAD + 1, :]
                part_out[j] = (accum[j, :HEAD, :] / total).astype(BF16)
                lse_out[j] = top[j] + jnp.log2(total)
                for copy in part_copy(j):
                    copy.start()

        return 0

    lax.fori_loop(0, 8, far, 0)

    for j in (1, 3, 2):
        remote(part_out.at[j], part_in.at[j], part_send.at[j], part_recv.at[j], partner).wait_recv()
        remote(lse_out.at[j], lse_in.at[j], lse_send.at[j], lse_recv.at[j], partner).wait_recv()

    best = jnp.maximum(jnp.maximum(top[0], lse_in[1]), jnp.maximum(lse_in[2], lse_in[3]))
    own_ratio = jnp.exp2(top[0] - best)
    ratios = [jnp.exp2(lse_in[j] - best) for j in (1, 2, 3)]
    total = accum[0, HEAD : HEAD + 1, :] * own_ratio + ratios[0] + ratios[1] + ratios[2]
    inverse = 1.0 / total
    own_ratio = own_ratio * inverse
    ratios = [r * inverse for r in ratios]
    for g in range(8):
        cols = slice(g * 128, (g + 1) * 128)
        summed = accum[0, :HEAD, cols] * own_ratio[:, cols]
        for j in (1, 2, 3):
            summed = summed + part_in[j, :, cols].astype(F32) * ratios[j - 1][:, cols]
        turned = summed.astype(BF16).T
        for n in range(2):
            here = slice((2 * g + n) * HEAD, (2 * g + n + 1) * HEAD)
            heads[:, here] = turned[n * 64 : (n + 1) * 64]
            gathered[0, core, :, here] = turned[n * 64 : (n + 1) * 64]

    def gather_copy(from_slot, dx, dy):
        slot = (from_slot // 4 + dx) * 4 + (from_slot % 4 + 4 - dy) % 4
        return remote(
            gathered.at[from_slot, core],
            gathered.at[slot, core],
            g_send.at[slot],
            g_recv.at[slot],
            peer(dx, dy, 0),
        )

    def onward(column):
        from_slot = column * 4 + 3 - 2 * core
        slot = column * 4 + 2
        return remote(
            gathered.at[from_slot, core],
            gathered.at[slot, core],
            g_send.at[slot],
            g_recv.at[slot],
            peer(0, 1 + 2 * core, 0),
        )

    def relay_copy(slot):
        return remote(
            gathered.at[slot, core],
            gathered.at[slot, core],
            relay_send.at[slot],
            relay_recv.at[slot],
            partner,
        )

    def arrived(slot):
        remote(
            gathered.at[0, core], gathered.at[slot, core], g_send.at[slot], g_recv.at[slot], partner
        ).wait_recv()
        relay_copy(slot).start()

    def row_block(slot):
        chip = (x + slot // 4) % 2 * 4 + (y + slot % 4) % 4
        return chip // 2, chip % 2

    def z_copy(slot):
        to_z, parity = row_block(slot)
        away = (z - to_z + 4) % 4
        return remote(
            sums_z.at[slot],
            z_in.at[away, parity],
            z_send.at[slot],
            z_recv.at[away, parity],
            (to_z * 2 + x_hi, grp, core),
        )

    def pair_copy(slot):
        return remote(
            sums_x.at[slot], pair_in.at[slot], pair_send.at[slot], pair_recv.at[slot], across
        )

    def multiply(slots):
        for slot in slots:
            remote(
                gathered.at[slot, core],
                gathered.at[slot, 1 - core],
                relay_send.at[slot],
                relay_recv.at[slot],
                partner,
            ).wait_recv()
        rows = jnp.concatenate([gathered[slot, n] for slot in slots for n in range(2)], axis=0)

        for part, (sums, start) in enumerate(((sums_x, Z_COLS), (sums_z, 0))):

            def columns(n, _, sums=sums, start=start):
                at = pl.ds(pl.multiple_of(n * 256, 256), 256)
                from_weight = pl.ds(pl.multiple_of(start + n * 256, 256), 256)
                value = jnp.dot(
                    rows, weight[:, from_weight], preferred_element_type=F32
                ).astype(BF16)
                for m, slot in enumerate(slots):
                    sums[slot, :, at] = value[m * 128 : (m + 1) * 128]
                return 0

            lax.fori_loop(0, sums.shape[2] // 256, columns, 0)
            for slot in slots:
                to_z, parity = row_block(slot)
                if part == 0:

                    @pl.when(parity != x_hi)
                    def _(slot=slot):
                        pair_copy(slot).start()

                else:

                    @pl.when(to_z != z)
                    def _(slot=slot):
                        z_copy(slot).start()

    def merge_slot(i):
        other = (y + x_hi) % 2
        return (1 - other) * ((i % 2) * 4 + (i // 2) * 2) + other * (2 * i + 1)

    def merged_copy(slot):
        to_z, _ = row_block(slot)
        return remote(
            merged.at[slot],
            merged_in.at[(z - to_z + 4) % 4],
            m_send.at[slot],
            m_recv.at[(z - to_z + 4) % 4],
            (to_z * 2 + x_hi, grp, core),
        )

    def merge(i):
        slot = merge_slot(i)
        remote(
            sums_x.at[slot], pair_in.at[slot], pair_send.at[slot], pair_recv.at[slot], across
        ).wait_recv()
        merged[slot] = (sums_x[slot].astype(F32) + pair_in[slot].astype(F32)).astype(BF16)
        to_z, _ = row_block(slot)

        @pl.when(to_z != z)
        def _():
            merged_copy(slot).start()

    relay_copy(0).start()
    for dx, dy in ((1, 0), (0, 1), (0, 3)):
        gather_copy(0, dx, dy).start()

    def gather_step(n):
        if n == 0:
            arrived(4)
            gather_copy(4, 0, 1).start()
            gather_copy(4, 0, 3).start()
        elif n == 1:
            arrived(1)
            arrived(3)
            onward(0).start()
        elif n == 2:
            arrived(5)
            arrived(7)
            onward(1).start()
        else:
            arrived(2)
            arrived(6)

    @pl.when(core == 0)
    def _():
        for n in range(4):
            gather_step(n)

    weight_copy.wait()
    for n, slots in enumerate(((0, 4), (1, 3), (5, 7), (2, 6))):

        @pl.when(core == 1)
        def _(n=n):
            gather_step(n)

        multiply(slots)
        if n >= 2:
            merge(2 * n - 4)
            merge(2 * n - 3)

    def own_slot(parity):
        chip = z * 2 + parity
        return (chip // 4 + x) % 2 * 4 + (chip % 4 - y + 4) % 4

    def z_total(parity):
        for away in (1, 2, 3):
            remote(
                sums_z.at[0], z_in.at[away, parity], z_send.at[0], z_recv.at[away, parity], partner
            ).wait_recv()
        total = sums_z[own_slot(parity)].astype(F32)
        for away in (1, 2, 3):
            total = total + z_in[away, parity].astype(F32)
        return total.astype(BF16)

    half_copy = remote(half_out, half_in, h_send, h_recv, across)
    half_out[...] = z_total(1 - x_hi)
    half_copy.start()
    out[:, :Z_COLS] = z_total(x_hi)
    for away in (1, 2, 3):
        remote(
            merged.at[0], merged_in.at[away], m_send.at[0], m_recv.at[away], partner
        ).wait_recv()
    total = merged[own_slot(x_hi)].astype(F32)
    for away in (1, 2, 3):
        total = total + merged_in[away].astype(F32)
    out[:, Z_COLS:] = total.astype(BF16)
    half_copy.wait_recv()

    half_copy.wait_send()
    for slot in range(8):
        relay_copy(slot).wait_send()
        to_z, parity = row_block(slot)

        @pl.when(to_z != z)
        def _():
            z_copy(slot).wait_send()

        @pl.when(parity != x_hi)
        def _():
            pair_copy(slot).wait_send()

        @pl.when((parity == x_hi) & (to_z != z))
        def _():
            merged_copy(slot).wait_send()

    for dx, dy in ((1, 0), (0, 1), (0, 3)):
        gather_copy(0, dx, dy).wait_send()
    for dy in (1, 3):
        gather_copy(4, 0, dy).wait_send()
    onward(0).wait_send()
    onward(1).wait_send()
    for slot in (1, 2, 3):
        kv_copy(slot).wait_send()
    for dy in (1, 3, 2):
        q_copy(dy).wait_send()
    for t in range(1, 4):
        for j in range(4):
            hist_copy(t, j).wait_send()
    for j in (1, 3, 2):
        for copy in part_copy(j):
            copy.wait_send()


def layer(blocks, lengths, new_k, new_v, queries, pre_k, pre_v, pool_k, pool_v, weight):
    dma = pltpu.SemaphoreType.DMA
    return pl.pallas_call(
        layer_kernel,
        out_shape=[
            jax.ShapeDtypeStruct((64, 2048), BF16),
            jax.ShapeDtypeStruct((128, 1024), BF16),
            jax.ShapeDtypeStruct((128, Z_COLS), BF16),
        ],
        in_specs=[VMEM] * 4 + [pl.BlockSpec(memory_space=pl.ANY)] * 6,
        out_specs=[VMEM] * 3,
        scratch_shapes=[
            pltpu.VMEM((64, 2048), BF16),
            pltpu.VMEM((8, 128, HEAD), BF16),
            pltpu.VMEM((32, 128, HEAD), BF16),
            pltpu.VMEM((32, 128, HEAD), BF16),
            pltpu.VMEM((8, 128), jnp.int32),
            pltpu.SMEM((8, 128), jnp.int32),
            dma((6,)),
            pltpu.VMEM((4, ROWS, HEAD), BF16),
            pltpu.VMEM((4, ROWS, 2 * HEAD), BF16),
            pltpu.VMEM((4, 2, 8, 128, 128), BF16),
            pltpu.VMEM((4, 4, 2, 2, 128, 128), BF16),
            pltpu.VMEM((4, 4, 2, 2, 128, 128), BF16),
            pltpu.VMEM((2, 128, 128), BF16),
            pltpu.VMEM((4, 1, ROWS), F32),
            pltpu.VMEM((4, HEAD + ONES, ROWS), F32),
            pltpu.VMEM((UNIT, TILE), F32),
            pltpu.VMEM((UNIT, TILE), F32),
            pltpu.VMEM((4, HEAD, ROWS), BF16),
            pltpu.VMEM((4, HEAD, ROWS), BF16),
            pltpu.VMEM((4, 1, ROWS), F32),
            pltpu.VMEM((4, 1, ROWS), F32),
            dma((4,)),
            dma((4,)),
            dma((4,)),
            dma((4,)),
            dma((4, 4)),
            dma((4, 4)),
            dma((4,)),
            dma((4,)),
            dma((4,)),
            dma((4,)),
            pltpu.VMEM((2048, 1024), BF16),
            pltpu.VMEM((8, 2, 64, 2048), BF16),
            pltpu.VMEM((8, 128, Z_COLS), BF16),
            pltpu.VMEM((8, 128, X_COLS), BF16),
            pltpu.VMEM((4, 2, 128, Z_COLS), BF16),
            pltpu.VMEM((8, 128, X_COLS), BF16),
            pltpu.VMEM((8, 128, X_COLS), BF16),
            pltpu.VMEM((4, 128, X_COLS), BF16),
            pltpu.VMEM((128, Z_COLS), BF16),
            dma,
            dma((8,)),
            dma((8,)),
            dma((8,)),
            dma((8,)),
            dma((8,)),
            dma((4, 2)),
            dma((8,)),
            dma((8,)),
            dma((8,)),
            dma((4,)),
            dma,
            dma,
        ],
        compiler_params=pltpu.CompilerParams(
            collective_id=0, has_side_effects=True, vmem_limit_bytes=VMEM_LIMIT
        ),
        name="layer",
    )(blocks, lengths, new_k, new_v, queries, pre_k, pre_v, pool_k, pool_v, weight)


def finish_kernel(heads_in, sums, half, heads, out):
    heads[...] = heads_in[...]
    out[:, Z_COLS:] = sums[:, Z_COLS:]
    out[:, :Z_COLS] = (sums[:, :Z_COLS].astype(F32) + half[...].astype(F32)).astype(BF16)


def finish(heads, sums, half):
    return pl.pallas_call(
        finish_kernel,
        out_shape=[jax.ShapeDtypeStruct(a.shape, a.dtype) for a in (heads, sums)],
        in_specs=[VMEM] * 3,
        out_specs=[VMEM] * 2,
        name="finish",
    )(heads, sums, half)


def on_device(
    queries,
    new_keys,
    new_values,
    prefix_keys,
    prefix_values,
    pool_keys,
    pool_values,
    hist_blocks,
    hist_len,
    out_weight,
):
    heads, sums, half = layer(
        hist_blocks.T,
        hist_len.reshape(1, -1),
        new_keys.reshape(64, HEAD),
        new_values.reshape(64, HEAD),
        queries.reshape(64, 2048),
        prefix_keys.reshape(8, 128, HEAD),
        prefix_values.reshape(8, 128, HEAD),
        pool_keys,
        pool_values,
        out_weight,
    )
    heads, projected = finish(heads, sums, half)
    return heads.reshape(2, 32, 2048), projected.reshape(4, 32, 1024)


def solution(mesh):
    in_specs = (
        P(("grp", "blk"), None, "kvh"),
        P(("grp", "blk"), None, "kvh"),
        P(("grp", "blk"), None, "kvh"),
        P(("grp", "blk"), "kvh"),
        P(("grp", "blk"), "kvh"),
        P(("grp", "blk"), None, "kvh"),
        P(("grp", "blk"), None, "kvh"),
        P(),
        P(),
        P("kvh", ("grp", "blk")),
    )
    out_specs = (P(("grp", "blk"), None, "kvh"), P("kvh", None, ("grp", "blk")))
    return jax.shard_map(
        on_device, mesh=mesh, in_specs=in_specs, out_specs=out_specs, check_vma=False
    )
```

```python
import functools
import math

import jax
import jax.numpy as jnp
from jax import lax
from jax.experimental import pallas as pl
from jax.experimental.pallas import tpu as pltpu
from jax.sharding import PartitionSpec as P

F32 = jnp.float32
BF16 = jnp.bfloat16
HEAD = 128
ROWS = 1024
TILE = 512
UNIT = 1024
ONES = 16
LOG2_SCALE = HEAD**-0.5 * math.log2(math.e)
HIDDEN = -1e30
NT = (((1,), (1,)), ((), ()))
Z_COLS = 512
X_COLS = 1024 - Z_COLS
VMEM_LIMIT = 60 * 2**20
VMEM = pl.BlockSpec(memory_space=pltpu.VMEM)


def place():
    kvh, grp, core = lax.axis_index("kvh"), lax.axis_index("grp"), lax.axis_index("blk")
    return kvh, grp // 4, grp % 4, core


def peer(dx, dy, dc):
    kvh, x, y, core = place()
    px = 1 - x if dx else x
    pc = 1 - core if dc else core
    return (kvh, px * 4 + (y + dy) % 4, pc)


def remote(src, dst, send, recv, to):
    return pltpu.make_async_remote_copy(
        src_ref=src,
        dst_ref=dst,
        send_sem=send,
        recv_sem=recv,
        device_id=to,
        device_id_type=pl.DeviceIdType.MESH,
    )


def turn(i):
    return jnp.where(i == 3, 0, 1 + (2 * i) % 3)


def layer_kernel(
    blocks,
    lengths,
    new_k,
    new_v,
    q_hbm,
    pre_k,
    pre_v,
    pool_k_hbm,
    pool_v_hbm,
    weight_in,
    heads,
    out,
    half_in,
    q_in,
    v_in,
    pool_k,
    pool_v,
    table_wide,
    table,
    in_sem,
    q_raw,
    q_two,
    kv,
    hist_out,
    hist,
    new_kv,
    top,
    accum,
    score_a,
    score_b,
    part_out,
    part_in,
    lse_out,
    lse_in,
    q_send,
    q_recv,
    kv_send,
    kv_recv,
    hist_send,
    hist_recv,
    part_send,
    part_recv,
    lse_send,
    lse_recv,
    weight,
    gathered,
    sums_z,
    sums_x,
    z_in,
    pair_in,
    merged,
    merged_in,
    half_out,
    w_sem,
    g_send,
    g_recv,
    relay_send,
    relay_recv,
    z_send,
    z_recv,
    pair_send,
    pair_recv,
    m_send,
    m_recv,
    h_send,
    h_recv,
):
    kvh, x, y, core = place()
    z, x_hi = kvh // 2, kvh % 2
    grp = x * 4 + y
    partner = peer(0, 0, 1)
    across = (z * 2 + 1 - x_hi, grp, core)
    weight_copy = pltpu.make_async_copy(weight_in, weight, w_sem)
    inputs = [
        pltpu.make_async_copy(src, dst, in_sem.at[n])
        for n, (src, dst) in enumerate(
            (
                (pre_k, kv.at[0, 0]),
                (pre_v, v_in),
                (q_hbm, q_in),
                (pool_k_hbm, pool_k),
                (pool_v_hbm, pool_v),
            )
        )
    ]
    for copy in inputs:
        copy.start()
    weight_copy.start()
    barrier = pltpu.get_barrier_semaphore()
    peers = [partner, peer(1, 0, 0), peer(1, 0, 1), peer(0, 1, 0), peer(0, 2, 0), peer(0, 3, 0), across]
    peers += [(((z + d) % 4) * 2 + x_hi, grp, core) for d in (1, 2, 3)]
    for to in peers:
        pl.semaphore_signal(barrier, inc=1, device_id=to, device_id_type=pl.DeviceIdType.MESH)
    scores = (score_a, score_b)

    def holder(t):
        dx, dc = t // 2, t % 2
        return ((1 - x if dx else x) * 4 + y) * 2 + (1 - core if dc else core)

    def fill_table():
        ids = blocks[...]
        request = lax.broadcasted_iota(jnp.int32, ids.shape, 1)
        block = lax.broadcasted_iota(jnp.int32, ids.shape, 0)
        live = jnp.clip(lengths[...] - 128 * block, 0, 128)
        code = ((request & 1) * 16 + block) * 16384 + live * 64 + (request & 1) * 32 + (ids & 31)
        for t in range(4):
            named = (ids >> 5) == holder(t)
            table_wide[2 * t : 2 * t + 1, :32] = jnp.min(
                jnp.where(named, code, 2**30), axis=0, keepdims=True
            )
            table_wide[2 * t + 1 : 2 * t + 2, :32] = jnp.max(
                jnp.where(named, code, -1), axis=0, keepdims=True
            )

    def entry(n, t, request_pair):
        one = table[2 * t + n, 2 * request_pair]
        two = table[2 * t + n, 2 * request_pair + 1]
        return jnp.maximum(one, two) if n else jnp.minimum(one, two)

    def score(j, keys, tile, mask):
        count = keys.shape[0]
        value = lax.dot_general(
            jnp.concatenate([keys, keys], axis=1),
            q_two[j, tile * TILE : (tile + 1) * TILE, :],
            NT,
            preferred_element_type=F32,
        )
        if mask is None:
            scores[tile][:count] = value
        else:
            for b in range(count // 128):
                rows = slice(b * 128, (b + 1) * 128)
                scores[tile][rows] = jnp.where(mask(b, tile), value[rows], HIDDEN)

    def weigh(j, values, tile, count):
        cols = slice(tile * TILE, (tile + 1) * TILE)
        old = top[j, :, cols]
        newest = jnp.maximum(old, scores[tile][:count].max(axis=0, keepdims=True))
        shrink = jnp.exp2(old - newest)
        top[j, :, cols] = newest
        weights = jnp.exp2(scores[tile][:count] - newest).astype(BF16)
        values = jnp.concatenate([values, jnp.ones((ONES, count), BF16)], axis=0)
        accum[j, :, cols] = accum[j, :, cols] * shrink + jnp.dot(
            values, weights, preferred_element_type=F32
        )

    def absorb(j, parts):
        tasks = [(part, tile) for part in parts for tile in range(2)]
        score(j, tasks[0][0][0](), tasks[0][1], tasks[0][0][2])
        for at, ((keys, values, mask), tile) in enumerate(tasks):
            if at + 1 < len(tasks):
                (after_keys, _, after_mask), after_tile = tasks[at + 1]
                score(j, after_keys(), after_tile, after_mask)
            loaded = values()
            weigh(j, loaded, tile, loaded.shape[1])

    def prefix_part(slot):
        return (
            lambda: jnp.concatenate([kv[slot, 0, b] for b in range(8)], axis=0),
            lambda: jnp.concatenate([kv[slot, 1, b] for b in range(8)], axis=1),
            None,
        )

    def hist_part(j):
        request_pair = (x * 4 + (y + j) % 4) * 2 + core

        def mask(b, tile):
            code = entry(b % 2, b // 2, request_pair)
            lane = lax.broadcasted_iota(jnp.int32, (1, TILE), 1)
            limit = jnp.where((lane // 32) % 2 == (code // 32) % 2, (code // 64) % 256, 0)
            return lax.broadcasted_iota(jnp.int32, (128, TILE), 0) < limit

        return (
            lambda: jnp.concatenate(
                [hist[t, j, 0, i] for t in range(4) for i in range(2)], axis=0
            ),
            lambda: jnp.concatenate(
                [hist[t, j, 1, i] for t in range(4) for i in range(2)], axis=1
            ),
            mask,
        )

    def new_part():
        def mask(b, tile):
            lane = lax.broadcasted_iota(jnp.int32, (128, TILE), 1) % 64
            key = lax.broadcasted_iota(jnp.int32, (128, TILE), 0)
            return (key <= lane) & (key >= (lane // 32) * 32)

        return (lambda: new_kv[0], lambda: new_kv[1], mask)

    def start_state(j):
        q = q_raw[j].astype(F32) * LOG2_SCALE
        high = q.astype(BF16)
        q_two[j, :, :HEAD] = high
        q_two[j, :, HEAD:] = (q - high.astype(F32)).astype(BF16)
        top[j] = jnp.full((1, ROWS), HIDDEN, F32)
        accum[j] = jnp.zeros((HEAD + ONES, ROWS), F32)

    fill_table()
    table_copy = pltpu.make_async_copy(table_wide, table, in_sem.at[5])
    table_copy.start()
    for copy in inputs[:3]:
        copy.wait()
    for b in range(8):
        kv[0, 1, b] = v_in[b].T
    for g in range(16):
        q_raw[0, g * 64 : (g + 1) * 64, :] = q_in[:, g * HEAD : (g + 1) * HEAD]
    pl.semaphore_wait(barrier, len(peers))

    def kv_copy(slot):
        src, to = ((0, partner), (0, peer(1, 0, 0)), (2, partner))[slot - 1]
        return remote(kv.at[src], kv.at[slot], kv_send.at[slot], kv_recv.at[slot], to)

    def q_copy(dy):
        to = peer(0, dy, 0)
        slot = (4 - dy) % 4
        return remote(q_raw.at[0], q_raw.at[slot], q_send.at[slot], q_recv.at[slot], to)

    def hist_copy(t, j):
        return remote(
            hist_out.at[t, j],
            hist.at[t, j],
            hist_send.at[t, j],
            hist_recv.at[t, j],
            (kvh, (x + t // 2) % 2 * 4 + y, (core + t % 2) % 2),
        )

    def part_copy(j):
        slot = (4 - j) % 4
        to = peer(0, j, 0)
        return (
            remote(part_out.at[j], part_in.at[slot], part_send.at[j], part_recv.at[slot], to),
            remote(lse_out.at[j], lse_in.at[slot], lse_send.at[j], lse_recv.at[slot], to),
        )

    kv_copy(2).start()
    kv_copy(1).start()
    for dy in (1, 3, 2):
        q_copy(dy).start()

    def gather_blocks(t, j, store):
        request_pair = ((x + t // 2) % 2 * 4 + (y + j) % 4) * 2 + (core + t % 2) % 2
        for n in range(2):
            local = entry(n, 0, request_pair) & 31
            store[t, j, 0, n] = pool_k[local]
            store[t, j, 1, n] = pool_v[local].T

    def send_along_x(lane):
        def fill(i, _):
            t, j = 2 + (core + lane) % 2, turn(i)
            gather_blocks(t, j, hist_out)
            hist_copy(t, j).start()
            return 0

        lax.fori_loop(0, 4, fill, 0)

    def send_near(i, _):
        j = turn(i)
        gather_blocks(1, j, hist_out)
        hist_copy(1, j).start()
        gather_blocks(0, j, hist)
        return 0

    for copy in inputs[3:]:
        copy.wait()
    table_copy.wait()
    send_along_x(0)
    send_along_x(1)
    lax.fori_loop(0, 4, send_near, 0)

    start_state(0)
    new_kv[...] = jnp.zeros((2, 128, 128), BF16)
    new_kv[0, :64, :] = new_k[...]
    new_kv[1, :, :] = jnp.concatenate([new_v[...], jnp.zeros((64, HEAD), BF16)], axis=0).T
    absorb(0, [prefix_part(0), new_part()])
    kv_copy(1).wait_recv()
    absorb(0, [prefix_part(1)])

    def near(i, _):
        @pl.when(i == 2)
        def _():
            kv_copy(2).wait_recv()
            kv_copy(3).start()

        j = turn(i)
        remote(q_raw.at[0], q_raw.at[j], q_send.at[j], q_recv.at[j], partner).wait_recv()
        start_state(j)
        absorb(j, [prefix_part(0), prefix_part(1)])
        return 0

    lax.fori_loop(0, 3, near, 0)
    kv_copy(3).wait_recv()

    def far(i, _):
        is_far = jnp.where(core == 0, 1 - i % 2, 1 - i // 4) == 1
        order = jnp.where(core == 0, i // 2, i % 4)
        j = turn(order)

        @pl.when(is_far)
        def _():
            absorb(j, [prefix_part(2), prefix_part(3)])

        @pl.when(jnp.logical_not(is_far))
        def _():
            for t in range(1, 4):
                hist_copy(t, j).wait_recv()
            absorb(j, [hist_part(j)])

            @pl.when(order < 3)
            def _():
                total = accum[j, HEAD : HEAD + 1, :]
                part_out[j] = (accum[j, :HEAD, :] / total).astype(BF16)
                lse_out[j] = top[j] + jnp.log2(total)
                for copy in part_copy(j):
                    copy.start()

        return 0

    lax.fori_loop(0, 8, far, 0)

    for j in (1, 3, 2):
        remote(part_out.at[j], part_in.at[j], part_send.at[j], part_recv.at[j], partner).wait_recv()
        remote(lse_out.at[j], lse_in.at[j], lse_send.at[j], lse_recv.at[j], partner).wait_recv()

    best = jnp.maximum(jnp.maximum(top[0], lse_in[1]), jnp.maximum(lse_in[2], lse_in[3]))
    own_ratio = jnp.exp2(top[0] - best)
    ratios = [jnp.exp2(lse_in[j] - best) for j in (1, 2, 3)]
    total = accum[0, HEAD : HEAD + 1, :] * own_ratio + ratios[0] + ratios[1] + ratios[2]
    inverse = 1.0 / total
    own_ratio = own_ratio * inverse
    ratios = [r * inverse for r in ratios]
    for g in range(8):
        cols = slice(g * 128, (g + 1) * 128)
        summed = accum[0, :HEAD, cols] * own_ratio[:, cols]
        for j in (1, 2, 3):
            summed = summed + part_in[j, :, cols].astype(F32) * ratios[j - 1][:, cols]
        turned = summed.astype(BF16).T
        for n in range(2):
            here = slice((2 * g + n) * HEAD, (2 * g + n + 1) * HEAD)
            heads[:, here] = turned[n * 64 : (n + 1) * 64]
            gathered[0, core, :, here] = turned[n * 64 : (n + 1) * 64]

    def gather_copy(from_slot, dx, dy):
        slot = (from_slot // 4 + dx) * 4 + (from_slot % 4 + 4 - dy) % 4
        return remote(
            gathered.at[from_slot, core],
            gathered.at[slot, core],
            g_send.at[slot],
            g_recv.at[slot],
            peer(dx, dy, 0),
        )

    def onward(column):
        from_slot = column * 4 + 3 - 2 * core
        slot = column * 4 + 2
        return remote(
            gathered.at[from_slot, core],
            gathered.at[slot, core],
            g_send.at[slot],
            g_recv.at[slot],
            peer(0, 1 + 2 * core, 0),
        )

    def relay_copy(slot):
        return remote(
            gathered.at[slot, core],
            gathered.at[slot, core],
            relay_send.at[slot],
            relay_recv.at[slot],
            partner,
        )

    def arrived(slot):
        remote(
            gathered.at[0, core], gathered.at[slot, core], g_send.at[slot], g_recv.at[slot], partner
        ).wait_recv()
        relay_copy(slot).start()

    def row_block(slot):
        chip = (x + slot // 4) % 2 * 4 + (y + slot % 4) % 4
        return chip // 2, chip % 2

    def z_copy(slot):
        to_z, parity = row_block(slot)
        away = (z - to_z + 4) % 4
        return remote(
            sums_z.at[slot],
            z_in.at[away, parity],
            z_send.at[slot],
            z_recv.at[away, parity],
            (to_z * 2 + x_hi, grp, core),
        )

    def pair_copy(slot):
        return remote(
            sums_x.at[slot], pair_in.at[slot], pair_send.at[slot], pair_recv.at[slot], across
        )

    def multiply(slots):
        for slot in slots:
            remote(
                gathered.at[slot, core],
                gathered.at[slot, 1 - core],
                relay_send.at[slot],
                relay_recv.at[slot],
                partner,
            ).wait_recv()
        rows = jnp.concatenate([gathered[slot, n] for slot in slots for n in range(2)], axis=0)

        for part, (sums, start) in enumerate(((sums_x, Z_COLS), (sums_z, 0))):

            def columns(n, _, sums=sums, start=start):
                at = pl.ds(pl.multiple_of(n * 512, 512), 512)
                from_weight = pl.ds(pl.multiple_of(start + n * 512, 512), 512)
                value = jnp.dot(
                    rows, weight[:, from_weight], preferred_element_type=F32
                ).astype(BF16)
                for m, slot in enumerate(slots):
                    sums[slot, :, at] = value[m * 128 : (m + 1) * 128]
                return 0

            lax.fori_loop(0, sums.shape[2] // 512, columns, 0)
            for slot in slots:
                to_z, parity = row_block(slot)
                if part == 0:

                    @pl.when(parity != x_hi)
                    def _(slot=slot):
                        pair_copy(slot).start()

                else:

                    @pl.when(to_z != z)
                    def _(slot=slot):
                        z_copy(slot).start()

    def merge_slot(i):
        other = (y + x_hi) % 2
        return (1 - other) * ((i % 2) * 4 + (i // 2) * 2) + other * (2 * i + 1)

    def merged_copy(slot):
        to_z, _ = row_block(slot)
        return remote(
            merged.at[slot],
            merged_in.at[(z - to_z + 4) % 4],
            m_send.at[slot],
            m_recv.at[(z - to_z + 4) % 4],
            (to_z * 2 + x_hi, grp, core),
        )

    def merge(i):
        slot = merge_slot(i)
        remote(
            sums_x.at[slot], pair_in.at[slot], pair_send.at[slot], pair_recv.at[slot], across
        ).wait_recv()
        merged[slot] = (sums_x[slot].astype(F32) + pair_in[slot].astype(F32)).astype(BF16)
        to_z, _ = row_block(slot)

        @pl.when(to_z != z)
        def _():
            merged_copy(slot).start()

    relay_copy(0).start()
    for dx, dy in ((1, 0), (0, 1), (0, 3)):
        gather_copy(0, dx, dy).start()

    def gather_step(n):
        if n == 0:
            arrived(4)
            gather_copy(4, 0, 1).start()
            gather_copy(4, 0, 3).start()
        elif n == 1:
            arrived(1)
            arrived(3)
            onward(0).start()
        elif n == 2:
            arrived(5)
            arrived(7)
            onward(1).start()
            arrived(2)
        else:
            arrived(6)

    @pl.when(core == 0)
    def _():
        for n in range(4):
            gather_step(n)

    weight_copy.wait()
    for n, slots in enumerate(((), (0, 4, 1, 3), (2, 5, 7), (6,))):

        @pl.when(core == 1)
        def _(n=n):
            gather_step(n)

        if slots:
            multiply(slots)
        if n >= 2:
            merge(2 * n - 4)
            merge(2 * n - 3)

    def own_slot(parity):
        chip = z * 2 + parity
        return (chip // 4 + x) % 2 * 4 + (chip % 4 - y + 4) % 4

    def z_total(parity):
        for away in (1, 2, 3):
            remote(
                sums_z.at[0], z_in.at[away, parity], z_send.at[0], z_recv.at[away, parity], partner
            ).wait_recv()
        total = sums_z[own_slot(parity)].astype(F32)
        for away in (1, 2, 3):
            total = total + z_in[away, parity].astype(F32)
        return total.astype(BF16)

    half_copy = remote(half_out, half_in, h_send, h_recv, across)
    half_out[...] = z_total(1 - x_hi)
    half_copy.start()
    out[:, :Z_COLS] = z_total(x_hi)
    for away in (1, 2, 3):
        remote(
            merged.at[0], merged_in.at[away], m_send.at[0], m_recv.at[away], partner
        ).wait_recv()
    total = merged[own_slot(x_hi)].astype(F32)
    for away in (1, 2, 3):
        total = total + merged_in[away].astype(F32)
    out[:, Z_COLS:] = total.astype(BF16)
    half_copy.wait_recv()

    half_copy.wait_send()
    for slot in range(8):
        relay_copy(slot).wait_send()
        to_z, parity = row_block(slot)

        @pl.when(to_z != z)
        def _():
            z_copy(slot).wait_send()

        @pl.when(parity != x_hi)
        def _():
            pair_copy(slot).wait_send()

        @pl.when((parity == x_hi) & (to_z != z))
        def _():
            merged_copy(slot).wait_send()

    for dx, dy in ((1, 0), (0, 1), (0, 3)):
        gather_copy(0, dx, dy).wait_send()
    for dy in (1, 3):
        gather_copy(4, 0, dy).wait_send()
    onward(0).wait_send()
    onward(1).wait_send()
    for slot in (1, 2, 3):
        kv_copy(slot).wait_send()
    for dy in (1, 3, 2):
        q_copy(dy).wait_send()
    for t in range(1, 4):
        for j in range(4):
            hist_copy(t, j).wait_send()
    for j in (1, 3, 2):
        for copy in part_copy(j):
            copy.wait_send()


def layer(blocks, lengths, new_k, new_v, queries, pre_k, pre_v, pool_k, pool_v, weight):
    dma = pltpu.SemaphoreType.DMA
    return pl.pallas_call(
        layer_kernel,
        out_shape=[
            jax.ShapeDtypeStruct((64, 2048), BF16),
            jax.ShapeDtypeStruct((128, 1024), BF16),
            jax.ShapeDtypeStruct((128, Z_COLS), BF16),
        ],
        in_specs=[VMEM] * 4 + [pl.BlockSpec(memory_space=pl.ANY)] * 6,
        out_specs=[VMEM] * 3,
        scratch_shapes=[
            pltpu.VMEM((64, 2048), BF16),
            pltpu.VMEM((8, 128, HEAD), BF16),
            pltpu.VMEM((32, 128, HEAD), BF16),
            pltpu.VMEM((32, 128, HEAD), BF16),
            pltpu.VMEM((8, 128), jnp.int32),
            pltpu.SMEM((8, 128), jnp.int32),
            dma((6,)),
            pltpu.VMEM((4, ROWS, HEAD), BF16),
            pltpu.VMEM((4, ROWS, 2 * HEAD), BF16),
            pltpu.VMEM((4, 2, 8, 128, 128), BF16),
            pltpu.VMEM((4, 4, 2, 2, 128, 128), BF16),
            pltpu.VMEM((4, 4, 2, 2, 128, 128), BF16),
            pltpu.VMEM((2, 128, 128), BF16),
            pltpu.VMEM((4, 1, ROWS), F32),
            pltpu.VMEM((4, HEAD + ONES, ROWS), F32),
            pltpu.VMEM((UNIT, TILE), F32),
            pltpu.VMEM((UNIT, TILE), F32),
            pltpu.VMEM((4, HEAD, ROWS), BF16),
            pltpu.VMEM((4, HEAD, ROWS), BF16),
            pltpu.VMEM((4, 1, ROWS), F32),
            pltpu.VMEM((4, 1, ROWS), F32),
            dma((4,)),
            dma((4,)),
            dma((4,)),
            dma((4,)),
            dma((4, 4)),
            dma((4, 4)),
            dma((4,)),
            dma((4,)),
            dma((4,)),
            dma((4,)),
            pltpu.VMEM((2048, 1024), BF16),
            pltpu.VMEM((8, 2, 64, 2048), BF16),
            pltpu.VMEM((8, 128, Z_COLS), BF16),
            pltpu.VMEM((8, 128, X_COLS), BF16),
            pltpu.VMEM((4, 2, 128, Z_COLS), BF16),
            pltpu.VMEM((8, 128, X_COLS), BF16),
            pltpu.VMEM((8, 128, X_COLS), BF16),
            pltpu.VMEM((4, 128, X_COLS), BF16),
            pltpu.VMEM((128, Z_COLS), BF16),
            dma,
            dma((8,)),
            dma((8,)),
            dma((8,)),
            dma((8,)),
            dma((8,)),
            dma((4, 2)),
            dma((8,)),
            dma((8,)),
            dma((8,)),
            dma((4,)),
            dma,
            dma,
        ],
        compiler_params=pltpu.CompilerParams(
            collective_id=0, has_side_effects=True, vmem_limit_bytes=VMEM_LIMIT
        ),
        name="layer",
    )(blocks, lengths, new_k, new_v, queries, pre_k, pre_v, pool_k, pool_v, weight)


def finish_kernel(heads_in, sums, half, heads, out):
    heads[...] = heads_in[...]
    out[:, Z_COLS:] = sums[:, Z_COLS:]
    out[:, :Z_COLS] = (sums[:, :Z_COLS].astype(F32) + half[...].astype(F32)).astype(BF16)


def finish(heads, sums, half):
    return pl.pallas_call(
        finish_kernel,
        out_shape=[jax.ShapeDtypeStruct(a.shape, a.dtype) for a in (heads, sums)],
        in_specs=[VMEM] * 3,
        out_specs=[VMEM] * 2,
        name="finish",
    )(heads, sums, half)


def on_device(
    queries,
    new_keys,
    new_values,
    prefix_keys,
    prefix_values,
    pool_keys,
    pool_values,
    hist_blocks,
    hist_len,
    out_weight,
):
    heads, sums, half = layer(
        hist_blocks.T,
        hist_len.reshape(1, -1),
        new_keys.reshape(64, HEAD),
        new_values.reshape(64, HEAD),
        queries.reshape(64, 2048),
        prefix_keys.reshape(8, 128, HEAD),
        prefix_values.reshape(8, 128, HEAD),
        pool_keys,
        pool_values,
        out_weight,
    )
    heads, projected = finish(heads, sums, half)
    return heads.reshape(2, 32, 2048), projected.reshape(4, 32, 1024)


def solution(mesh):
    in_specs = (
        P(("grp", "blk"), None, "kvh"),
        P(("grp", "blk"), None, "kvh"),
        P(("grp", "blk"), None, "kvh"),
        P(("grp", "blk"), "kvh"),
        P(("grp", "blk"), "kvh"),
        P(("grp", "blk"), None, "kvh"),
        P(("grp", "blk"), None, "kvh"),
        P(),
        P(),
        P("kvh", ("grp", "blk")),
    )
    out_specs = (P(("grp", "blk"), None, "kvh"), P("kvh", None, ("grp", "blk")))
    return jax.shard_map(
        on_device, mesh=mesh, in_specs=in_specs, out_specs=out_specs, check_vma=False
    )
```

```python
import functools
import math

import jax
import jax.numpy as jnp
from jax import lax
from jax.experimental import pallas as pl
from jax.experimental.pallas import tpu as pltpu
from jax.sharding import PartitionSpec as P

F32 = jnp.float32
BF16 = jnp.bfloat16
HEAD = 128
ROWS = 1024
TILE = 512
UNIT = 1024
ONES = 16
LOG2_SCALE = HEAD**-0.5 * math.log2(math.e)
HIDDEN = -1e30
NT = (((1,), (1,)), ((), ()))
Z_COLS = 512
X_COLS = 1024 - Z_COLS
VMEM_LIMIT = 60 * 2**20
VMEM = pl.BlockSpec(memory_space=pltpu.VMEM)


def place():
    kvh, grp, core = lax.axis_index("kvh"), lax.axis_index("grp"), lax.axis_index("blk")
    return kvh, grp // 4, grp % 4, core


def peer(dx, dy, dc):
    kvh, x, y, core = place()
    px = 1 - x if dx else x
    pc = 1 - core if dc else core
    return (kvh, px * 4 + (y + dy) % 4, pc)


def remote(src, dst, send, recv, to):
    return pltpu.make_async_remote_copy(
        src_ref=src,
        dst_ref=dst,
        send_sem=send,
        recv_sem=recv,
        device_id=to,
        device_id_type=pl.DeviceIdType.MESH,
    )


def turn(i):
    return jnp.where(i == 3, 0, 1 + (2 * i) % 3)


def layer_kernel(
    blocks,
    lengths,
    new_k,
    new_v,
    q_hbm,
    pre_k,
    pre_v,
    pool_k_hbm,
    pool_v_hbm,
    weight_in,
    heads,
    out,
    half_in,
    q_in,
    v_in,
    pool_k,
    pool_v,
    table_wide,
    table,
    in_sem,
    q_raw,
    q_two,
    kv,
    hist_out,
    hist,
    new_kv,
    top,
    accum,
    score_a,
    score_b,
    part_out,
    part_in,
    lse_out,
    lse_in,
    q_send,
    q_recv,
    kv_send,
    kv_recv,
    hist_send,
    hist_recv,
    part_send,
    part_recv,
    lse_send,
    lse_recv,
    weight,
    gathered,
    sums_z,
    sums_x,
    z_in,
    pair_in,
    merged,
    merged_in,
    half_out,
    w_sem,
    g_send,
    g_recv,
    relay_send,
    relay_recv,
    z_send,
    z_recv,
    pair_send,
    pair_recv,
    m_send,
    m_recv,
    h_send,
    h_recv,
):
    kvh, x, y, core = place()
    z, x_hi = kvh // 2, kvh % 2
    grp = x * 4 + y
    partner = peer(0, 0, 1)
    across = (z * 2 + 1 - x_hi, grp, core)
    weight_copy = pltpu.make_async_copy(weight_in, weight, w_sem)
    inputs = [
        pltpu.make_async_copy(src, dst, in_sem.at[n])
        for n, (src, dst) in enumerate(
            (
                (pre_k, kv.at[0, 0]),
                (pre_v, v_in),
                (q_hbm, q_in),
                (pool_k_hbm, pool_k),
                (pool_v_hbm, pool_v),
            )
        )
    ]
    for copy in inputs:
        copy.start()
    weight_copy.start()
    barrier = pltpu.get_barrier_semaphore()
    peers = [partner, peer(1, 0, 0), peer(1, 0, 1), peer(0, 1, 0), peer(0, 2, 0), peer(0, 3, 0), across]
    peers += [(((z + d) % 4) * 2 + x_hi, grp, core) for d in (1, 2, 3)]
    for to in peers:
        pl.semaphore_signal(barrier, inc=1, device_id=to, device_id_type=pl.DeviceIdType.MESH)
    scores = (score_a, score_b)

    def holder(t):
        dx, dc = t // 2, t % 2
        return ((1 - x if dx else x) * 4 + y) * 2 + (1 - core if dc else core)

    def fill_table():
        ids = blocks[...]
        request = lax.broadcasted_iota(jnp.int32, ids.shape, 1)
        block = lax.broadcasted_iota(jnp.int32, ids.shape, 0)
        live = jnp.clip(lengths[...] - 128 * block, 0, 128)
        code = ((request & 1) * 16 + block) * 16384 + live * 64 + (request & 1) * 32 + (ids & 31)
        for t in range(4):
            named = (ids >> 5) == holder(t)
            table_wide[2 * t : 2 * t + 1, :32] = jnp.min(
                jnp.where(named, code, 2**30), axis=0, keepdims=True
            )
            table_wide[2 * t + 1 : 2 * t + 2, :32] = jnp.max(
                jnp.where(named, code, -1), axis=0, keepdims=True
            )

    def entry(n, t, request_pair):
        one = table[2 * t + n, 2 * request_pair]
        two = table[2 * t + n, 2 * request_pair + 1]
        return jnp.maximum(one, two) if n else jnp.minimum(one, two)

    def score(j, keys, tile, mask):
        count = keys.shape[0]
        value = lax.dot_general(
            jnp.concatenate([keys, keys], axis=1),
            q_two[j, tile * TILE : (tile + 1) * TILE, :],
            NT,
            preferred_element_type=F32,
        )
        if mask is None:
            scores[tile][:count] = value
        else:
            for b in range(count // 128):
                rows = slice(b * 128, (b + 1) * 128)
                scores[tile][rows] = jnp.where(mask(b, tile), value[rows], HIDDEN)

    def weigh(j, values, tile, count):
        cols = slice(tile * TILE, (tile + 1) * TILE)
        old = top[j, :, cols]
        newest = jnp.maximum(old, scores[tile][:count].max(axis=0, keepdims=True))
        shrink = jnp.exp2(old - newest)
        top[j, :, cols] = newest
        weights = jnp.exp2(scores[tile][:count] - newest).astype(BF16)
        values = jnp.concatenate([values, jnp.ones((ONES, count), BF16)], axis=0)
        accum[j, :, cols] = accum[j, :, cols] * shrink + jnp.dot(
            values, weights, preferred_element_type=F32
        )

    def absorb(j, parts):
        tasks = [(part, tile) for part in parts for tile in range(2)]
        score(j, tasks[0][0][0](), tasks[0][1], tasks[0][0][2])
        for at, ((keys, values, mask), tile) in enumerate(tasks):
            if at + 1 < len(tasks):
                (after_keys, _, after_mask), after_tile = tasks[at + 1]
                score(j, after_keys(), after_tile, after_mask)
            loaded = values()
            weigh(j, loaded, tile, loaded.shape[1])

    def prefix_part(slot):
        return (
            lambda: jnp.concatenate([kv[slot, 0, b] for b in range(8)], axis=0),
            lambda: jnp.concatenate([kv[slot, 1, b] for b in range(8)], axis=1),
            None,
        )

    def hist_part(j):
        request_pair = (x * 4 + (y + j) % 4) * 2 + core

        def mask(b, tile):
            code = entry(b % 2, b // 2, request_pair)
            lane = lax.broadcasted_iota(jnp.int32, (1, TILE), 1)
            limit = jnp.where((lane // 32) % 2 == (code // 32) % 2, (code // 64) % 256, 0)
            return lax.broadcasted_iota(jnp.int32, (128, TILE), 0) < limit

        return (
            lambda: jnp.concatenate(
                [hist[t, j, 0, i] for t in range(4) for i in range(2)], axis=0
            ),
            lambda: jnp.concatenate(
                [hist[t, j, 1, i] for t in range(4) for i in range(2)], axis=1
            ),
            mask,
        )

    def new_part():
        def mask(b, tile):
            lane = lax.broadcasted_iota(jnp.int32, (128, TILE), 1) % 64
            key = lax.broadcasted_iota(jnp.int32, (128, TILE), 0)
            return (key <= lane) & (key >= (lane // 32) * 32)

        return (lambda: new_kv[0], lambda: new_kv[1], mask)

    def start_state(j):
        q = q_raw[j].astype(F32) * LOG2_SCALE
        high = q.astype(BF16)
        q_two[j, :, :HEAD] = high
        q_two[j, :, HEAD:] = (q - high.astype(F32)).astype(BF16)
        top[j] = jnp.full((1, ROWS), HIDDEN, F32)
        accum[j] = jnp.zeros((HEAD + ONES, ROWS), F32)

    fill_table()
    table_copy = pltpu.make_async_copy(table_wide, table, in_sem.at[5])
    table_copy.start()
    for copy in inputs[:3]:
        copy.wait()
    for b in range(8):
        kv[0, 1, b] = v_in[b].T
    for g in range(16):
        q_raw[0, g * 64 : (g + 1) * 64, :] = q_in[:, g * HEAD : (g + 1) * HEAD]
    pl.semaphore_wait(barrier, len(peers))

    def kv_copy(slot):
        src, to = ((0, partner), (0, peer(1, 0, 0)), (2, partner))[slot - 1]
        return remote(kv.at[src], kv.at[slot], kv_send.at[slot], kv_recv.at[slot], to)

    def q_copy(dy):
        to = peer(0, dy, 0)
        slot = (4 - dy) % 4
        return remote(q_raw.at[0], q_raw.at[slot], q_send.at[slot], q_recv.at[slot], to)

    def hist_copy(t, j):
        return remote(
            hist_out.at[t, j],
            hist.at[t, j],
            hist_send.at[t, j],
            hist_recv.at[t, j],
            (kvh, (x + t // 2) % 2 * 4 + y, (core + t % 2) % 2),
        )

    def part_copy(j):
        slot = (4 - j) % 4
        to = peer(0, j, 0)
        return (
            remote(part_out.at[j], part_in.at[slot], part_send.at[j], part_recv.at[slot], to),
            remote(lse_out.at[j], lse_in.at[slot], lse_send.at[j], lse_recv.at[slot], to),
        )

    kv_copy(2).start()
    kv_copy(1).start()
    for dy in (1, 3, 2):
        q_copy(dy).start()

    def gather_blocks(t, j, store):
        request_pair = ((x + t // 2) % 2 * 4 + (y + j) % 4) * 2 + (core + t % 2) % 2
        for n in range(2):
            local = entry(n, 0, request_pair) & 31
            store[t, j, 0, n] = pool_k[local]
            store[t, j, 1, n] = pool_v[local].T

    def send_along_x(lane):
        def fill(i, _):
            t, j = 2 + (core + lane) % 2, turn(i)
            gather_blocks(t, j, hist_out)
            hist_copy(t, j).start()
            return 0

        lax.fori_loop(0, 4, fill, 0)

    def send_near(i, _):
        j = turn(i)
        gather_blocks(1, j, hist_out)
        hist_copy(1, j).start()
        gather_blocks(0, j, hist)
        return 0

    for copy in inputs[3:]:
        copy.wait()
    table_copy.wait()
    send_along_x(0)
    send_along_x(1)
    lax.fori_loop(0, 4, send_near, 0)

    start_state(0)
    new_kv[...] = jnp.zeros((2, 128, 128), BF16)
    new_kv[0, :64, :] = new_k[...]
    new_kv[1, :, :] = jnp.concatenate([new_v[...], jnp.zeros((64, HEAD), BF16)], axis=0).T
    absorb(0, [prefix_part(0), new_part()])
    kv_copy(1).wait_recv()
    absorb(0, [prefix_part(1)])

    def near(i, _):
        @pl.when(i == 2)
        def _():
            kv_copy(2).wait_recv()
            kv_copy(3).start()

        j = turn(i)
        remote(q_raw.at[0], q_raw.at[j], q_send.at[j], q_recv.at[j], partner).wait_recv()
        start_state(j)
        absorb(j, [prefix_part(0), prefix_part(1)])
        return 0

    lax.fori_loop(0, 3, near, 0)
    kv_copy(3).wait_recv()

    def far(i, _):
        is_far = jnp.where(core == 0, 1 - i % 2, 1 - i // 4) == 1
        order = jnp.where(core == 0, i // 2, i % 4)
        j = turn(order)

        @pl.when(is_far)
        def _():
            absorb(j, [prefix_part(2), prefix_part(3)])

        @pl.when(jnp.logical_not(is_far))
        def _():
            for t in range(1, 4):
                hist_copy(t, j).wait_recv()
            absorb(j, [hist_part(j)])

            @pl.when(order < 3)
            def _():
                total = accum[j, HEAD : HEAD + 1, :]
                part_out[j] = (accum[j, :HEAD, :] / total).astype(BF16)
                lse_out[j] = top[j] + jnp.log2(total)
                for copy in part_copy(j):
                    copy.start()

        return 0

    lax.fori_loop(0, 8, far, 0)

    for j in (1, 3, 2):
        remote(part_out.at[j], part_in.at[j], part_send.at[j], part_recv.at[j], partner).wait_recv()
        remote(lse_out.at[j], lse_in.at[j], lse_send.at[j], lse_recv.at[j], partner).wait_recv()

    best = jnp.maximum(jnp.maximum(top[0], lse_in[1]), jnp.maximum(lse_in[2], lse_in[3]))
    own_ratio = jnp.exp2(top[0] - best)
    ratios = [jnp.exp2(lse_in[j] - best) for j in (1, 2, 3)]
    total = accum[0, HEAD : HEAD + 1, :] * own_ratio + ratios[0] + ratios[1] + ratios[2]
    inverse = 1.0 / total
    own_ratio = own_ratio * inverse
    ratios = [r * inverse for r in ratios]
    for g in range(8):
        cols = slice(g * 128, (g + 1) * 128)
        summed = accum[0, :HEAD, cols] * own_ratio[:, cols]
        for j in (1, 2, 3):
            summed = summed + part_in[j, :, cols].astype(F32) * ratios[j - 1][:, cols]
        turned = summed.astype(BF16).T
        for n in range(2):
            here = slice((2 * g + n) * HEAD, (2 * g + n + 1) * HEAD)
            heads[:, here] = turned[n * 64 : (n + 1) * 64]
            gathered[0, core, :, here] = turned[n * 64 : (n + 1) * 64]

    def gather_copy(from_slot, dx, dy):
        slot = (from_slot // 4 + dx) * 4 + (from_slot % 4 + 4 - dy) % 4
        return remote(
            gathered.at[from_slot, core],
            gathered.at[slot, core],
            g_send.at[slot],
            g_recv.at[slot],
            peer(dx, dy, 0),
        )

    def onward(column):
        from_slot = column * 4 + 3 - 2 * core
        slot = column * 4 + 2
        return remote(
            gathered.at[from_slot, core],
            gathered.at[slot, core],
            g_send.at[slot],
            g_recv.at[slot],
            peer(0, 1 + 2 * core, 0),
        )

    def relay_copy(slot):
        return remote(
            gathered.at[slot, core],
            gathered.at[slot, core],
            relay_send.at[slot],
            relay_recv.at[slot],
            partner,
        )

    def arrived(slot):
        remote(
            gathered.at[0, core], gathered.at[slot, core], g_send.at[slot], g_recv.at[slot], partner
        ).wait_recv()
        relay_copy(slot).start()

    def row_block(slot):
        chip = (x + slot // 4) % 2 * 4 + (y + slot % 4) % 4
        return chip // 2, chip % 2

    def z_copy(slot):
        to_z, parity = row_block(slot)
        away = (z - to_z + 4) % 4
        return remote(
            sums_z.at[slot],
            z_in.at[away, parity],
            z_send.at[slot],
            z_recv.at[away, parity],
            (to_z * 2 + x_hi, grp, core),
        )

    def pair_copy(slot):
        return remote(
            sums_x.at[slot], pair_in.at[slot], pair_send.at[slot], pair_recv.at[slot], across
        )

    def multiply(slots):
        for slot in slots:
            remote(
                gathered.at[slot, core],
                gathered.at[slot, 1 - core],
                relay_send.at[slot],
                relay_recv.at[slot],
                partner,
            ).wait_recv()
        rows = jnp.concatenate([gathered[slot, n] for slot in slots for n in range(2)], axis=0)

        for part, (sums, start) in enumerate(((sums_x, Z_COLS), (sums_z, 0))):

            def columns(n, _, sums=sums, start=start):
                at = pl.ds(pl.multiple_of(n * 512, 512), 512)
                from_weight = pl.ds(pl.multiple_of(start + n * 512, 512), 512)
                value = jnp.dot(
                    rows, weight[:, from_weight], preferred_element_type=F32
                ).astype(BF16)
                for m, slot in enumerate(slots):
                    sums[slot, :, at] = value[m * 128 : (m + 1) * 128]
                return 0

            lax.fori_loop(0, sums.shape[2] // 512, columns, 0)
            for slot in slots:
                to_z, parity = row_block(slot)
                if part == 0:

                    @pl.when(parity != x_hi)
                    def _(slot=slot):
                        pair_copy(slot).start()

                else:

                    @pl.when(to_z != z)
                    def _(slot=slot):
                        z_copy(slot).start()

    def merge_slot(i):
        other = (y + x_hi) % 2
        return (1 - other) * ((i % 2) * 4 + (i // 2) * 2) + other * (2 * i + 1)

    def merged_copy(slot):
        to_z, _ = row_block(slot)
        return remote(
            merged.at[slot],
            merged_in.at[(z - to_z + 4) % 4],
            m_send.at[slot],
            m_recv.at[(z - to_z + 4) % 4],
            (to_z * 2 + x_hi, grp, core),
        )

    def merge(i):
        slot = merge_slot(i)
        remote(
            sums_x.at[slot], pair_in.at[slot], pair_send.at[slot], pair_recv.at[slot], across
        ).wait_recv()
        merged[slot] = (sums_x[slot].astype(F32) + pair_in[slot].astype(F32)).astype(BF16)
        to_z, _ = row_block(slot)

        @pl.when(to_z != z)
        def _():
            merged_copy(slot).start()

    relay_copy(0).start()
    for dx, dy in ((1, 0), (0, 1), (0, 3)):
        gather_copy(0, dx, dy).start()

    def gather_step(n):
        if n == 0:
            arrived(4)
            gather_copy(4, 0, 1).start()
            gather_copy(4, 0, 3).start()
        elif n == 1:
            arrived(1)
            arrived(3)
            onward(0).start()
        elif n == 2:
            arrived(5)
            arrived(7)
            onward(1).start()
            arrived(2)
        else:
            arrived(6)

    @pl.when(core == 0)
    def _():
        for n in range(4):
            gather_step(n)

    weight_copy.wait()
    for n, slots in enumerate(((), (0, 4, 1, 3), (2, 5, 7), (6,))):

        @pl.when(core == 1)
        def _(n=n):
            gather_step(n)

        if slots:
            multiply(slots)
        if n == 2:
            merge(0)
            merge(1)

    def own_slot(parity):
        chip = z * 2 + parity
        return (chip // 4 + x) % 2 * 4 + (chip % 4 - y + 4) % 4

    def z_total(parity):
        for away in (1, 2, 3):
            remote(
                sums_z.at[0], z_in.at[away, parity], z_send.at[0], z_recv.at[away, parity], partner
            ).wait_recv()
        total = sums_z[own_slot(parity)].astype(F32)
        for away in (1, 2, 3):
            total = total + z_in[away, parity].astype(F32)
        return total.astype(BF16)

    half_copy = remote(half_out, half_in, h_send, h_recv, across)
    last_is_own = (y + x_hi) % 2 == 0

    def send_half():
        half_out[...] = z_total(1 - x_hi)
        half_copy.start()

    @pl.when(last_is_own)
    def _():
        send_half()
        merge(2)
        merge(3)

    @pl.when(jnp.logical_not(last_is_own))
    def _():
        merge(2)
        merge(3)
        send_half()

    out[:, :Z_COLS] = z_total(x_hi)
    for away in (1, 2, 3):
        remote(
            merged.at[0], merged_in.at[away], m_send.at[0], m_recv.at[away], partner
        ).wait_recv()
    total = merged[own_slot(x_hi)].astype(F32)
    for away in (1, 2, 3):
        total = total + merged_in[away].astype(F32)
    out[:, Z_COLS:] = total.astype(BF16)
    half_copy.wait_recv()

    half_copy.wait_send()
    for slot in range(8):
        relay_copy(slot).wait_send()
        to_z, parity = row_block(slot)

        @pl.when(to_z != z)
        def _():
            z_copy(slot).wait_send()

        @pl.when(parity != x_hi)
        def _():
            pair_copy(slot).wait_send()

        @pl.when((parity == x_hi) & (to_z != z))
        def _():
            merged_copy(slot).wait_send()

    for dx, dy in ((1, 0), (0, 1), (0, 3)):
        gather_copy(0, dx, dy).wait_send()
    for dy in (1, 3):
        gather_copy(4, 0, dy).wait_send()
    onward(0).wait_send()
    onward(1).wait_send()
    for slot in (1, 2, 3):
        kv_copy(slot).wait_send()
    for dy in (1, 3, 2):
        q_copy(dy).wait_send()
    for t in range(1, 4):
        for j in range(4):
            hist_copy(t, j).wait_send()
    for j in (1, 3, 2):
        for copy in part_copy(j):
            copy.wait_send()


def layer(blocks, lengths, new_k, new_v, queries, pre_k, pre_v, pool_k, pool_v, weight):
    dma = pltpu.SemaphoreType.DMA
    return pl.pallas_call(
        layer_kernel,
        out_shape=[
            jax.ShapeDtypeStruct((64, 2048), BF16),
            jax.ShapeDtypeStruct((128, 1024), BF16),
            jax.ShapeDtypeStruct((128, Z_COLS), BF16),
        ],
        in_specs=[VMEM] * 4 + [pl.BlockSpec(memory_space=pl.ANY)] * 6,
        out_specs=[VMEM] * 3,
        scratch_shapes=[
            pltpu.VMEM((64, 2048), BF16),
            pltpu.VMEM((8, 128, HEAD), BF16),
            pltpu.VMEM((32, 128, HEAD), BF16),
            pltpu.VMEM((32, 128, HEAD), BF16),
            pltpu.VMEM((8, 128), jnp.int32),
            pltpu.SMEM((8, 128), jnp.int32),
            dma((6,)),
            pltpu.VMEM((4, ROWS, HEAD), BF16),
            pltpu.VMEM((4, ROWS, 2 * HEAD), BF16),
            pltpu.VMEM((4, 2, 8, 128, 128), BF16),
            pltpu.VMEM((4, 4, 2, 2, 128, 128), BF16),
            pltpu.VMEM((4, 4, 2, 2, 128, 128), BF16),
            pltpu.VMEM((2, 128, 128), BF16),
            pltpu.VMEM((4, 1, ROWS), F32),
            pltpu.VMEM((4, HEAD + ONES, ROWS), F32),
            pltpu.VMEM((UNIT, TILE), F32),
            pltpu.VMEM((UNIT, TILE), F32),
            pltpu.VMEM((4, HEAD, ROWS), BF16),
            pltpu.VMEM((4, HEAD, ROWS), BF16),
            pltpu.VMEM((4, 1, ROWS), F32),
            pltpu.VMEM((4, 1, ROWS), F32),
            dma((4,)),
            dma((4,)),
            dma((4,)),
            dma((4,)),
            dma((4, 4)),
            dma((4, 4)),
            dma((4,)),
            dma((4,)),
            dma((4,)),
            dma((4,)),
            pltpu.VMEM((2048, 1024), BF16),
            pltpu.VMEM((8, 2, 64, 2048), BF16),
            pltpu.VMEM((8, 128, Z_COLS), BF16),
            pltpu.VMEM((8, 128, X_COLS), BF16),
            pltpu.VMEM((4, 2, 128, Z_COLS), BF16),
            pltpu.VMEM((8, 128, X_COLS), BF16),
            pltpu.VMEM((8, 128, X_COLS), BF16),
            pltpu.VMEM((4, 128, X_COLS), BF16),
            pltpu.VMEM((128, Z_COLS), BF16),
            dma,
            dma((8,)),
            dma((8,)),
            dma((8,)),
            dma((8,)),
            dma((8,)),
            dma((4, 2)),
            dma((8,)),
            dma((8,)),
            dma((8,)),
            dma((4,)),
            dma,
            dma,
        ],
        compiler_params=pltpu.CompilerParams(
            collective_id=0, has_side_effects=True, vmem_limit_bytes=VMEM_LIMIT
        ),
        name="layer",
    )(blocks, lengths, new_k, new_v, queries, pre_k, pre_v, pool_k, pool_v, weight)


def finish_kernel(heads_in, sums, half, heads, out):
    heads[...] = heads_in[...]
    out[:, Z_COLS:] = sums[:, Z_COLS:]
    out[:, :Z_COLS] = (sums[:, :Z_COLS].astype(F32) + half[...].astype(F32)).astype(BF16)


def finish(heads, sums, half):
    return pl.pallas_call(
        finish_kernel,
        out_shape=[jax.ShapeDtypeStruct(a.shape, a.dtype) for a in (heads, sums)],
        in_specs=[VMEM] * 3,
        out_specs=[VMEM] * 2,
        name="finish",
    )(heads, sums, half)


def on_device(
    queries,
    new_keys,
    new_values,
    prefix_keys,
    prefix_values,
    pool_keys,
    pool_values,
    hist_blocks,
    hist_len,
    out_weight,
):
    heads, sums, half = layer(
        hist_blocks.T,
        hist_len.reshape(1, -1),
        new_keys.reshape(64, HEAD),
        new_values.reshape(64, HEAD),
        queries.reshape(64, 2048),
        prefix_keys.reshape(8, 128, HEAD),
        prefix_values.reshape(8, 128, HEAD),
        pool_keys,
        pool_values,
        out_weight,
    )
    heads, projected = finish(heads, sums, half)
    return heads.reshape(2, 32, 2048), projected.reshape(4, 32, 1024)


def solution(mesh):
    in_specs = (
        P(("grp", "blk"), None, "kvh"),
        P(("grp", "blk"), None, "kvh"),
        P(("grp", "blk"), None, "kvh"),
        P(("grp", "blk"), "kvh"),
        P(("grp", "blk"), "kvh"),
        P(("grp", "blk"), None, "kvh"),
        P(("grp", "blk"), None, "kvh"),
        P(),
        P(),
        P("kvh", ("grp", "blk")),
    )
    out_specs = (P(("grp", "blk"), None, "kvh"), P("kvh", None, ("grp", "blk")))
    return jax.shard_map(
        on_device, mesh=mesh, in_specs=in_specs, out_specs=out_specs, check_vma=False
    )
```
